32 devices in a mesh: row: 8 (over z, core), col: 4 (over y, x).
Axes of the slice: x: 2, y: 2, z: 4, core: 2. Of those that a mesh axis runs over, the one named last changes fastest.
Arguments:
- rhs: float32 [8, 1024, 1024], P('row', None, 'col'), may hold values from -6 to 6
- panel: float32 [8, 2, 1024, 1024], P('row', None, 'col'), may hold values from -0.125 to 0.125
- diag_inverse: float32 [2, 1024, 1024], P(None, 'row'), as said below
- flags: int32 [8, 2], P('row'), may hold values 0 or 1
- slot_block: int32 [8], replicated, may hold values from 0 to 7, each once
Outputs:
- result: float32 [8, 1024, 1024], P('row', None, 'col')
The draws below stay inside these ranges and needn't reach their ends.
Inputs may be any that keep to these rules, and one draw needn't show every extreme that they name: `slot_block`: each block row 0 to 7 is held by exactly one slot. `diag_inverse`: lower triangular with a positive diagonal.
All inputs are finite; a program needn't handle non-finite values. No bound on the sum of `flags` on one device may be relied on, other than what follows from the above.
Results may differ from the reference program's by a relative error of at most 0.000078.
Values sent between devices are 32-bit elements; how exact they have to be, the bound alone decides.
No kernel may reach another device: no remote copies, remote signals or barrier semaphores. Data moves between devices by JAX's collectives and lax.ppermute only.
A program may use at most 64 MiB of HBM per device.

```python
import math
import jax
import jax.numpy as jnp
from jax import lax

NB = 1024
NBLK = 8
NRHS = 1024


def draw_diag_inverse(key, part):
    key = jax.random.fold_in(key, 5)
    key_low, key_diag = jax.random.split(key)
    rows = lax.broadcasted_iota(jnp.int32, (2, NB, NB), 1)
    cols = lax.broadcasted_iota(jnp.int32, (2, NB, NB), 2)
    lower = jax.random.normal(key_low, (2, NB, NB), jnp.float32) * (1.5 / math.sqrt(NB))
    middle = jax.random.uniform(key_diag, (2, NB, NB), jnp.float32, 1.0, 2.0)
    return jnp.where(rows > cols, lower, jnp.where(rows == cols, middle, 0.0)).astype(jnp.float32)


def touch_ends(result, stream_key, low, top_value):
    spot = [jax.random.randint(jax.random.fold_in(stream_key, axis), (), 0, length) for axis, length in enumerate(result.shape)]
    main_axis = result.shape.index(max(result.shape))
    next_to = spot[:main_axis] + [(spot[main_axis] + 1) % result.shape[main_axis]] + spot[main_axis + 1:]
    return result.at[tuple(spot)].set(low).at[tuple(next_to)].set(top_value)


def block_levels(own_key, extent, pieces, least, high):
    def one(position, shards_of):
        draws = jax.random.uniform(jax.random.fold_in(jax.random.fold_in(own_key, 6), position), (shards_of,), jnp.float32, least / len(pieces), high / len(pieces))
        return jnp.repeat(jnp.exp(draws), extent[position] // shards_of).reshape((-1,) + (1,) * (len(extent) - position - 1))

    gain = one(*pieces[0])
    for cut in pieces[1:]:
        gain = gain * one(*cut)
    return gain


def scatter_about(key, extent, width, reach, cuts=(), dtype=jnp.bfloat16):
    values = width * jax.random.normal(key, extent, jnp.float32)
    if cuts:
        values = values * block_levels(key, extent, cuts, -0.22, 0.18)
    return jnp.clip(values, -reach, reach).astype(dtype)


def setup_inputs(seed: int = 0) -> dict:
    arg_keys = jax.random.split(jax.random.key(seed), 6)
    rhs = scatter_about(arg_keys[0], (NBLK, NB, NRHS), 1.0, 6.0, ((0, 8), (2, 4)), jnp.float32)
    panel = scatter_about(arg_keys[1], (NBLK, 2, NB, NB), (2 * NB) ** -0.5, 0.125, ((0, 8), (2, 4)), jnp.float32)
    diag_inverse = draw_diag_inverse(jax.random.fold_in(arg_keys[5], 71), 0)
    flags = touch_ends((jax.random.randint(arg_keys[3], (NBLK, 2), 0, 4) < 3).astype(jnp.int32), jax.random.fold_in(arg_keys[3], 1), 0, 1)
    slot_block = jax.random.permutation(arg_keys[4], NBLK).astype(jnp.int32)
    return {"rhs": rhs, "panel": panel, "diag_inverse": diag_inverse, "flags": flags, "slot_block": slot_block}


def reference(rhs, panel, diag_inverse, flags, slot_block):
    highest = lax.Precision.HIGHEST
    weights = flags.astype(jnp.float32)
    slot_zero = jnp.argmax(slot_block == 0).astype(jnp.int32)
    slot_one = jnp.argmax(slot_block == 1).astype(jnp.int32)
    solved0 = jnp.dot(diag_inverse[0], rhs[slot_zero], precision=highest)
    first = rhs - weights[:, 0][:, None, None] * jnp.einsum("sij,jr->sir", panel[:, 0], solved0, precision=highest)
    solved1 = jnp.dot(diag_inverse[1], first[slot_one], precision=highest)
    second = first - weights[:, 1][:, None, None] * jnp.einsum("sij,jr->sir", panel[:, 1], solved1, precision=highest)
    is_zero = (slot_block == 0)[:, None, None]
    is_one = (slot_block == 1)[:, None, None]
    return jnp.where(is_zero, solved0[None], jnp.where(is_one, solved1[None], second))
```

```python
import functools

import jax
import jax.numpy as jnp
from jax import lax
from jax.experimental import pallas as pl
from jax.experimental.pallas import tpu as pltpu
from jax.sharding import PartitionSpec as P

HIGH = lax.Precision.HIGH


def bit(index, b):
    return (index >> b) & 1


def swap(x, axis, b, size):
    return lax.ppermute(x, axis, [(i, i ^ (1 << b)) for i in range(size)])


def tie(value, *others):
    return lax.optimization_barrier((value, *others))


def join(low_first, a, b):
    return jnp.where(low_first, jnp.concatenate([a, b]), jnp.concatenate([b, a]))


def halves(x, b):
    half = x.shape[0] // 2
    return lax.dynamic_slice_in_dim(x, b * half, half), lax.dynamic_slice_in_dim(x, (1 - b) * half, half)


def scatter_step(x, b, size, owner, me):
    mine = bit(me, b)
    keep, send = halves(x, mine)
    return jnp.where(bit(owner, b) == mine, keep, swap(send, "row", b, size))


def cross_step(x, b, size, owner, me):
    return jnp.where(bit(owner, b) == bit(me, b), x, swap(x, "row", b, size))


def gather_step(x, b, size, me):
    return join(bit(me, b) == 0, x, swap(x, "row", b, size))


def split(x):
    high = x.astype(jnp.bfloat16)
    return high, (x - high.astype(jnp.float32)).astype(jnp.bfloat16)


def dot3(a, b):
    def dot(p, q):
        return jnp.dot(p, q, preferred_element_type=jnp.float32)

    return dot(a[0], b[0]) + (dot(a[0], b[1]) + dot(a[1], b[0]))


def prepare_body(step, ids, own, *refs):
    pieces, (high, low, panel, sems) = refs[:6], refs[6:]
    side = ids[1]
    half = pieces[0].shape[0]
    sources = [(own.at[0, step], side * 2)]
    for ref, (distance, part) in zip(pieces, ((1, 0), (2, 1), (1, 1), (2, 0), (3, 0), (3, 1))):
        sources.append((ref, (side ^ distance) * 2 + part))
    copies = []
    for index, (ref, place) in enumerate(sources):
        rows = pl.ds(pl.multiple_of(place * half, half), ref.shape[0])
        copy = pltpu.make_async_copy(ref, panel.at[rows], sems.at[index])
        copy.start()
        copies.append(copy)
    for copy in copies:
        copy.wait()
    for start in range(0, panel.shape[0], half):
        rows = pl.ds(start, half)
        high[rows], low[rows] = split(panel[rows])


def prepare(ids, panel, step, pieces):
    depth = panel.shape[3]
    vmem, anywhere = pl.BlockSpec(memory_space=pltpu.VMEM), pl.BlockSpec(memory_space=pl.ANY)
    return pl.pallas_call(
        functools.partial(prepare_body, step),
        out_shape=[jax.ShapeDtypeStruct((depth, depth), jnp.bfloat16)] * 2,
        in_specs=[pl.BlockSpec(memory_space=pltpu.SMEM)] + [anywhere] * 7,
        out_specs=[vmem] * 2,
        scratch_shapes=[pltpu.VMEM((depth, depth), jnp.float32), pltpu.SemaphoreType.DMA((7,))],
        compiler_params=pltpu.CompilerParams(vmem_limit_bytes=8 * 2**20),
        cost_estimate=pl.CostEstimate(flops=0, bytes_accessed=8 * depth * depth, transcendentals=0),
        name="prepare",
    )(ids, panel, *pieces)


def update_body(step, ids, weight, high, low, own_x, other_x, current, out, *rest):
    x = rest[-1]
    rank, held = ids[0], ids[2]
    core, z = bit(rank, 0), rank >> 1
    share = own_x.shape[0] // 4
    for distance in range(4):
        block = pl.ds(distance * share, share)
        place = (z ^ distance) * 2
        x[pl.ds(pl.multiple_of((place + core) * share, share), share)] = own_x[block]
        x[pl.ds(pl.multiple_of((place + 1 - core) * share, share), share)] = other_x[block]
    parts = split(x[...])
    size = out.shape[0] // 2
    for start in (0, size):
        rows = pl.ds(start, size)
        new = current[rows] - weight[0] * dot3((high[rows], low[rows]), parts)
        if step == 0:
            out[rows] = jnp.where(held == 0, x[rows], new)
        else:
            out[rows] = jnp.where(held == 0, current[rows], jnp.where(held == 1, x[rows], new))
    if step == 0:
        rest[0][...] = out[pl.ds(pl.multiple_of((1 - core) * size, size), size)]


def update(step, ids, weight, pair, own_x, other_x, current):
    rows, cols = current.shape
    depth = pair[0].shape[1]
    vmem, smem = pl.BlockSpec(memory_space=pltpu.VMEM), pl.BlockSpec(memory_space=pltpu.SMEM)
    counts = (rows, rows // 2) if step == 0 else (rows,)
    return pl.pallas_call(
        functools.partial(update_body, step),
        out_shape=[jax.ShapeDtypeStruct((count, cols), jnp.float32) for count in counts],
        in_specs=[smem, smem] + [vmem] * 5,
        out_specs=[vmem] * len(counts),
        scratch_shapes=[pltpu.VMEM((depth, cols), jnp.float32)],
        compiler_params=pltpu.CompilerParams(vmem_limit_bytes=8 * 2**20),
        cost_estimate=pl.CostEstimate(flops=6 * rows * depth * cols, bytes_accessed=4 * rows * (depth + 3 * cols), transcendentals=0),
        name="update",
    )(ids, weight, *pair, own_x, other_x, current)


def general(rows, cols, rhs, panel, diag_inverse, flags, slot_block):
    rank = lax.axis_index("row")
    owners = (jnp.argmax(slot_block == 0), jnp.argmax(slot_block == 1))
    weights = flags[0].astype(jnp.float32)
    bits = rows.bit_length() - 1
    current = rhs[0]
    solved = []
    for step in range(2):
        pivot = current
        for b in range(bits - 1):
            pivot = scatter_step(pivot, b, rows, owners[step], rank)
        pivot = cross_step(pivot, bits - 1, rows, owners[step], rank)
        for b in reversed(range(bits - 1)):
            pivot = gather_step(pivot, b, rows, rank)
        x = jnp.dot(diag_inverse[step], pivot, precision=HIGH)
        for b in range(bits):
            x = gather_step(x, b, rows, rank)
        whole = lax.all_gather(panel[0, step], "col", axis=0, tiled=True)
        current = current - weights[step] * jnp.dot(whole, x, precision=HIGH)
        solved.append(x)
    held = slot_block[rank]
    return jnp.where(held == 0, solved[0], jnp.where(held == 1, solved[1], current))[None]


def paced(rows, cols, rhs, panel, diag_inverse, flags, slot_block):
    rank, side = lax.axis_index("row"), lax.axis_index("col")
    owner = jnp.argmax(slot_block == 0)
    half = panel.shape[2] // 2
    core = bit(rank, 0)

    def near(one, two):
        return [swap(one, "col", 0, cols), swap(two, "col", 1, cols)]

    def far(one, two):
        return [swap(one, "col", 1, cols), swap(two, "col", 0, cols)]

    def block_halves(panel, step):
        return panel[0, step, :half], panel[0, step, half:]

    y = scatter_step(rhs[0], 0, rows, owner, rank)
    y, panel = tie(y, panel)
    top, bottom = block_halves(panel, 0)
    first0 = near(top, bottom)
    y = scatter_step(y, 1, rows, owner, rank)
    y, panel, flags, slot_block, rank_, side_ = tie(y, panel, flags, slot_block, rank, side)
    top, bottom = block_halves(panel, 0)
    second0 = near(bottom, top)
    weights = flags[0].astype(jnp.float32)
    ids = jnp.stack([rank_, side_, slot_block[rank_]])
    second = jnp.argmax(slot_block == 1)
    y = cross_step(y, 2, rows, owner, rank)
    y, ids, weight0, weight1, second, *first0 = tie(y, ids, weights[0:1], weights[1:2], second, *first0)
    far0 = far(*first0)
    y = gather_step(y, 1, rows, rank)
    y, *second0 = tie(y, *second0)
    other = swap(y, "row", 0, rows)
    other, *far0 = tie(other, *far0)
    y = join(core == 0, y, other)
    x = jnp.dot(diag_inverse[0], y, precision=HIGH)
    x2, x1 = swap(x, "row", 2, rows), swap(x, "row", 1, rows)
    x2, x1 = tie(x2, x1)
    pair = prepare(ids, panel, 0, [*first0, *second0, *far0])
    x3 = swap(x2, "row", 1, rows)
    x3, high, low = tie(x3, *pair)
    x = jnp.concatenate([x, x1, x2, x3])
    other = swap(x, "row", 0, rows)
    current, send = update(0, ids, weight0, (high, low), x, other, rhs[0])
    got = swap(send, "row", 0, rows)
    keep = lax.dynamic_slice_in_dim(current, core * send.shape[0], send.shape[0])
    y = jnp.where(bit(second, 0) == core, keep, got)
    y, panel = tie(y, panel)
    top, bottom = block_halves(panel, 1)
    first1 = near(top, bottom)
    y = scatter_step(y, 1, rows, second, rank)
    y, panel = tie(y, panel)
    top, bottom = block_halves(panel, 1)
    second1 = near(bottom, top)
    y = cross_step(y, 2, rows, second, rank)
    y, *first1 = tie(y, *first1)
    far1 = far(*first1)
    y = gather_step(y, 1, rows, rank)
    y, *second1 = tie(y, *second1)
    other = swap(y, "row", 0, rows)
    other, *far1 = tie(other, *far1)
    y = join(core == 0, y, other)
    x = jnp.dot(diag_inverse[1], y, precision=HIGH)
    x2, x1 = swap(x, "row", 2, rows), swap(x, "row", 1, rows)
    pair = prepare(ids, panel, 1, [*first1, *second1, *far1])
    x2, x1, *pair = tie(x2, x1, *pair)
    x3 = swap(x2, "row", 1, rows)
    x = jnp.concatenate([x, x1, x2, x3])
    other = swap(x, "row", 0, rows)
    (result,) = update(1, ids, weight1, pair, x, other, current)
    return result[None]


def solution(mesh):
    rows, cols = mesh.shape["row"], mesh.shape["col"]
    form = paced if (rows, cols) == (8, 4) else general

    def shards(*args):
        return form(rows, cols, *args)

    in_specs = (
        P("row", None, "col"),
        P("row", None, "col", None),
        P(None, "row", None),
        P("row", None),
        P(),
    )
    out_specs = P("row", None, "col")
    return jax.shard_map(shards, mesh=mesh, in_specs=in_specs, out_specs=out_specs, check_vma=False)
```

```python
import functools

import jax
import jax.numpy as jnp
from jax import lax
from jax.experimental import pallas as pl
from jax.experimental.pallas import tpu as pltpu
from jax.sharding import PartitionSpec as P

HIGH = lax.Precision.HIGH
PREPARE_BYTES = 4 * 2**20
UPDATE_BYTES = 5 * 2**20


def bit(index, b):
    return (index >> b) & 1


def swap(x, axis, b, size):
    return lax.ppermute(x, axis, [(i, i ^ (1 << b)) for i in range(size)])


def tie(value, *others):
    return lax.optimization_barrier((value, *others))


def join(low_first, a, b):
    return jnp.where(low_first, jnp.concatenate([a, b]), jnp.concatenate([b, a]))


def halves(x, b):
    half = x.shape[0] // 2
    return lax.dynamic_slice_in_dim(x, b * half, half), lax.dynamic_slice_in_dim(x, (1 - b) * half, half)


def scatter_step(x, b, size, owner, me):
    mine = bit(me, b)
    keep, send = halves(x, mine)
    return jnp.where(bit(owner, b) == mine, keep, swap(send, "row", b, size))


def cross_step(x, b, size, owner, me):
    return jnp.where(bit(owner, b) == bit(me, b), x, swap(x, "row", b, size))


def gather_step(x, b, size, me):
    return join(bit(me, b) == 0, x, swap(x, "row", b, size))


def split(x):
    high = x.astype(jnp.bfloat16)
    return high, (x - high.astype(jnp.float32)).astype(jnp.bfloat16)


def dot3(a, b):
    def dot(p, q):
        return jnp.dot(p, q, preferred_element_type=jnp.float32)

    return dot(a[0], b[0]) + (dot(a[0], b[1]) + dot(a[1], b[0]))


def prepare_body(own_top, own_bottom, *refs):
    pieces, (high, low, slots, sems) = refs[:6], refs[6:]
    side = lax.axis_index("col")
    half = pieces[0].shape[0]
    sources = [(own_top, side * 2), (own_bottom, side * 2 + 1)]
    for ref, (distance, part) in zip(pieces, ((1, 0), (2, 1), (1, 1), (2, 0), (3, 0), (3, 1))):
        sources.append((ref, (side ^ distance) * 2 + part))
    groups = [sources[start:start + 2] for start in range(0, 8, 2)]

    def fetch(index):
        copies = []
        start = 0
        for member, (ref, _) in enumerate(groups[index]):
            into = slots.at[index % 2, pl.ds(start, ref.shape[0])]
            copies.append(pltpu.make_async_copy(ref, into, sems.at[index % 2, member]))
            start += ref.shape[0]
        for copy in copies:
            copy.start()
        return copies

    flying = [fetch(0), fetch(1)]
    for index, group in enumerate(groups):
        for copy in flying[index]:
            copy.wait()
        start = 0
        for ref, place in group:
            rows = pl.ds(pl.multiple_of(place * half, half), ref.shape[0])
            high[rows], low[rows] = split(slots[index % 2, pl.ds(start, ref.shape[0])])
            start += ref.shape[0]
        if index + 2 < len(groups):
            flying.append(fetch(index + 2))


def prepare(pieces):
    half, depth = pieces[0].shape
    vmem, anywhere = pl.BlockSpec(memory_space=pltpu.VMEM), pl.BlockSpec(memory_space=pl.ANY)
    return pl.pallas_call(
        prepare_body,
        out_shape=[jax.ShapeDtypeStruct((depth, depth), jnp.bfloat16)] * 2,
        in_specs=[anywhere] * 8,
        out_specs=[vmem] * 2,
        scratch_shapes=[pltpu.VMEM((2, 2 * half, depth), jnp.float32), pltpu.SemaphoreType.DMA((2, 2))],
        compiler_params=pltpu.CompilerParams(vmem_limit_bytes=PREPARE_BYTES),
        cost_estimate=pl.CostEstimate(flops=0, bytes_accessed=16 * depth * depth, transcendentals=0),
        name="prepare",
    )(*pieces)


def assemble(x, blocks, rank):
    core, z = bit(rank, 0), rank >> 1
    share = blocks[0].shape[0]
    for index, ref in enumerate(blocks):
        place = (z ^ (index & 3)) * 2 + (core ^ (index >> 2))
        x[pl.ds(pl.multiple_of(place * share, share), share)] = ref[...]


def first_body(flags, slot_block, high, low, *refs):
    blocks, (rhs, keep, send, x, current, sem) = refs[:8], refs[8:]
    copy = pltpu.make_async_copy(rhs.at[0], current, sem)
    copy.start()
    rank = lax.axis_index("row")
    core = bit(rank, 0)
    assemble(x, blocks, rank)
    parts = split(x[...])
    weight = flags[0, 0].astype(jnp.float32)
    size = keep.shape[0]
    copy.wait()
    for out, part in ((send, 1 - core), (keep, core)):
        rows = pl.ds(pl.multiple_of(part * size, size), size)
        new = current[rows] - weight * dot3((high[rows], low[rows]), parts)
        out[...] = jnp.where(slot_block[rank] == 0, x[rows], new)


def second_body(flags, slot_block, high, low, *refs):
    blocks, (keep, send, out, x) = refs[:8], refs[8:]
    rank = lax.axis_index("row")
    core, held = bit(rank, 0), slot_block[rank]
    assemble(x, blocks, rank)
    parts = split(x[...])
    weight = flags[0, 1].astype(jnp.float32)
    size = keep.shape[0]
    for current, part in ((keep, core), (send, 1 - core)):
        rows = pl.ds(pl.multiple_of(part * size, size), size)
        new = current[...] - weight * dot3((high[rows], low[rows]), parts)
        out[rows] = jnp.where(held == 0, current[...], jnp.where(held == 1, x[rows], new))


def solve_body(step, inverse, *refs):
    quarters, (out, y) = refs[:4], refs[4:]
    rank = lax.axis_index("row")
    size = quarters[0].shape[0]
    core, z = bit(rank, 0), bit(rank, 1)
    for index, ref in enumerate(quarters):
        place = (core ^ (index >> 1)) * 2 + (z ^ (index & 1))
        y[pl.ds(pl.multiple_of(place * size, size), size)] = ref[...]
    out[...] = dot3(split(inverse[step]), split(y[...]))


def solve(step, inverse, quarters):
    _, rows, depth = inverse.shape
    cols = quarters[0].shape[1]
    vmem = pl.BlockSpec(memory_space=pltpu.VMEM)
    return pl.pallas_call(
        functools.partial(solve_body, step),
        out_shape=jax.ShapeDtypeStruct((rows, cols), jnp.float32),
        in_specs=[vmem] * 5,
        out_specs=vmem,
        scratch_shapes=[pltpu.VMEM((depth, cols), jnp.float32)],
        compiler_params=pltpu.CompilerParams(vmem_limit_bytes=UPDATE_BYTES),
        cost_estimate=pl.CostEstimate(flops=6 * rows * depth * cols, bytes_accessed=4 * (rows * depth + depth * cols), transcendentals=0),
        name="solve",
    )(inverse, *quarters)


def update(step, flags, slot_block, pair, blocks, current):
    depth = pair[0].shape[1]
    rows, cols = pair[0].shape[0], blocks[0].shape[1]
    vmem, smem = pl.BlockSpec(memory_space=pltpu.VMEM), pl.BlockSpec(memory_space=pltpu.SMEM)
    counts = (rows // 2, rows // 2) if step == 0 else (rows,)
    scratch = [pltpu.VMEM((depth, cols), jnp.float32)]
    if step == 0:
        scratch += [pltpu.VMEM((rows, cols), jnp.float32), pltpu.SemaphoreType.DMA]
    return pl.pallas_call(
        first_body if step == 0 else second_body,
        out_shape=[jax.ShapeDtypeStruct((count, cols), jnp.float32) for count in counts],
        in_specs=[smem, smem] + [vmem] * 10 + ([pl.BlockSpec(memory_space=pl.ANY)] if step == 0 else [vmem] * 2),
        out_specs=[vmem] * len(counts),
        scratch_shapes=scratch,
        compiler_params=pltpu.CompilerParams(vmem_limit_bytes=UPDATE_BYTES),
        cost_estimate=pl.CostEstimate(flops=6 * rows * depth * cols, bytes_accessed=4 * rows * (depth + 3 * cols), transcendentals=0),
        name="update",
    )(flags, slot_block, *pair, *blocks, *current)


def general(rows, cols, rhs, panel, diag_inverse, flags, slot_block):
    rank = lax.axis_index("row")
    owners = (jnp.argmax(slot_block == 0), jnp.argmax(slot_block == 1))
    weights = flags[0].astype(jnp.float32)
    bits = rows.bit_length() - 1
    current = rhs[0]
    solved = []
    for step in range(2):
        pivot = current
        for b in range(bits - 1):
            pivot = scatter_step(pivot, b, rows, owners[step], rank)
        pivot = cross_step(pivot, bits - 1, rows, owners[step], rank)
        for b in reversed(range(bits - 1)):
            pivot = gather_step(pivot, b, rows, rank)
        x = jnp.dot(diag_inverse[step], pivot, precision=HIGH)
        for b in range(bits):
            x = gather_step(x, b, rows, rank)
        whole = lax.all_gather(panel[0, step], "col", axis=0, tiled=True)
        current = current - weights[step] * jnp.dot(whole, x, precision=HIGH)
        solved.append(x)
    held = slot_block[rank]
    return jnp.where(held == 0, solved[0], jnp.where(held == 1, solved[1], current))[None]


def paced(rows, cols, rhs, panel, diag_inverse, flags, slot_block):
    rank = lax.axis_index("row")
    owner, second = jnp.argmax(slot_block == 0), jnp.argmax(slot_block == 1)
    half = panel.shape[2] // 2
    core = bit(rank, 0)

    def near(one, two):
        return [swap(one, "col", 0, cols), swap(two, "col", 1, cols)]

    def far(one, two):
        return [swap(one, "col", 1, cols), swap(two, "col", 0, cols)]

    def solved(step, y, block, first, owner):
        y = scatter_step(y, 1, rows, owner, rank)
        y, top, bottom = tie(y, *block)
        second = near(bottom, top)
        y = cross_step(y, 2, rows, owner, rank)
        y, *first = tie(y, *first)
        pieces = far(*first)
        other = swap(y, "row", 0, rows)
        beside = swap(y, "row", 1, rows)
        beside, other, *second = tie(beside, other, *second)
        last = swap(beside, "row", 0, rows)
        x = solve(step, diag_inverse, [y, beside, other, last])
        x2, x1 = swap(x, "row", 2, rows), swap(x, "row", 1, rows)
        x2, x1, *pieces = tie(x2, x1, *pieces)
        high, low = prepare([*block, *first, *second, *pieces])
        x3 = swap(x2, "row", 1, rows)
        across = [swap(part, "row", 0, rows) for part in (x, x1, x2)]
        x3, high, low, *across = tie(x3, high, low, *across)
        return [x, x1, x2, x3, *across, swap(x3, "row", 0, rows)], (high, low)

    y = scatter_step(rhs[0], 0, rows, owner, rank)
    y, panel = tie(y, panel)
    cut = [panel[0, step, start:start + half] for step in range(2) for start in (0, half)]
    cut = lax.optimization_barrier(cut)
    blocks, pair = solved(0, y, cut[:2], near(*cut[:2]), owner)
    first = near(*cut[2:])
    keep, send = update(0, flags, slot_block, pair, blocks, [rhs])
    keep, send, *first = tie(keep, send, *first)
    got = swap(send, "row", 0, rows)
    y = jnp.where(bit(second, 0) == core, keep, got)
    blocks, pair = solved(1, y, cut[2:], first, second)
    (result,) = update(1, flags, slot_block, pair, blocks, [keep, send])
    return result[None]


def solution(mesh):
    rows, cols = mesh.shape["row"], mesh.shape["col"]
    form = paced if (rows, cols) == (8, 4) else general

    def shards(*args):
        return form(rows, cols, *args)

    in_specs = (
        P("row", None, "col"),
        P("row", None, "col", None),
        P(None, "row", None),
        P("row", None),
        P(),
    )
    out_specs = P("row", None, "col")
    return jax.shard_map(shards, mesh=mesh, in_specs=in_specs, out_specs=out_specs, check_vma=False)
```

```python
import functools

import jax
import jax.numpy as jnp
from jax import lax
from jax.experimental import pallas as pl
from jax.experimental.pallas import tpu as pltpu
from jax.sharding import PartitionSpec as P

HIGH = lax.Precision.HIGH
PREPARE_BYTES = 4 * 2**20
UPDATE_BYTES = 5 * 2**20


def bit(index, b):
    return (index >> b) & 1


def swap(x, axis, b, size):
    return lax.ppermute(x, axis, [(i, i ^ (1 << b)) for i in range(size)])


def tie(value, *others):
    return lax.optimization_barrier((value, *others))


def join(low_first, a, b):
    return jnp.where(low_first, jnp.concatenate([a, b]), jnp.concatenate([b, a]))


def halves(x, b):
    half = x.shape[0] // 2
    return lax.dynamic_slice_in_dim(x, b * half, half), lax.dynamic_slice_in_dim(x, (1 - b) * half, half)


def scatter_step(x, b, size, owner, me):
    mine = bit(me, b)
    keep, send = halves(x, mine)
    return jnp.where(bit(owner, b) == mine, keep, swap(send, "row", b, size))


def cross_step(x, b, size, owner, me):
    return jnp.where(bit(owner, b) == bit(me, b), x, swap(x, "row", b, size))


def gather_step(x, b, size, me):
    return join(bit(me, b) == 0, x, swap(x, "row", b, size))


def split(x):
    high = x.astype(jnp.bfloat16)
    return high, (x - high.astype(jnp.float32)).astype(jnp.bfloat16)


def dot3(a, b):
    def dot(p, q):
        return jnp.dot(p, q, preferred_element_type=jnp.float32)

    return dot(a[0], b[0]) + (dot(a[0], b[1]) + dot(a[1], b[0]))


def prepare_body(step, own, *refs):
    pieces, (high, low, slots, sems) = refs[:6], refs[6:]
    side = lax.axis_index("col")
    half = pieces[0].shape[0]
    sources = [(own.at[0, step], side * 2)]
    for ref, (distance, part) in zip(pieces, ((1, 0), (2, 1), (1, 1), (2, 0), (3, 0), (3, 1))):
        sources.append((ref, (side ^ distance) * 2 + part))
    groups = [sources[0:1], sources[1:3], sources[3:5], sources[5:7]]

    def fetch(index):
        copies = []
        start = 0
        for member, (ref, _) in enumerate(groups[index]):
            into = slots.at[index % 2, pl.ds(start, ref.shape[0])]
            copies.append(pltpu.make_async_copy(ref, into, sems.at[index % 2, member]))
            start += ref.shape[0]
        for copy in copies:
            copy.start()
        return copies

    flying = [fetch(0), fetch(1)]
    for index, group in enumerate(groups):
        for copy in flying[index]:
            copy.wait()
        start = 0
        for ref, place in group:
            rows = pl.ds(pl.multiple_of(place * half, half), ref.shape[0])
            high[rows], low[rows] = split(slots[index % 2, pl.ds(start, ref.shape[0])])
            start += ref.shape[0]
        if index + 2 < len(groups):
            flying.append(fetch(index + 2))


def prepare(panel, step, pieces):
    depth = panel.shape[3]
    vmem, anywhere = pl.BlockSpec(memory_space=pltpu.VMEM), pl.BlockSpec(memory_space=pl.ANY)
    return pl.pallas_call(
        functools.partial(prepare_body, step),
        out_shape=[jax.ShapeDtypeStruct((depth, depth), jnp.bfloat16)] * 2,
        in_specs=[anywhere] * 7,
        out_specs=[vmem] * 2,
        scratch_shapes=[pltpu.VMEM((2, panel.shape[2], depth), jnp.float32), pltpu.SemaphoreType.DMA((2, 2))],
        compiler_params=pltpu.CompilerParams(vmem_limit_bytes=PREPARE_BYTES),
        cost_estimate=pl.CostEstimate(flops=0, bytes_accessed=16 * depth * depth, transcendentals=0),
        name="prepare",
    )(panel, *pieces)


def assemble(x, blocks, rank):
    core, z = bit(rank, 0), rank >> 1
    share = blocks[0].shape[0]
    for index, ref in enumerate(blocks):
        place = (z ^ (index & 3)) * 2 + (core ^ (index >> 2))
        x[pl.ds(pl.multiple_of(place * share, share), share)] = ref[...]


def first_body(flags, slot_block, high, low, *refs):
    blocks, (rhs, keep, send, x, current, sem) = refs[:8], refs[8:]
    copy = pltpu.make_async_copy(rhs.at[0], current, sem)
    copy.start()
    rank = lax.axis_index("row")
    core = bit(rank, 0)
    assemble(x, blocks, rank)
    parts = split(x[...])
    weight = flags[0, 0].astype(jnp.float32)
    size = keep.shape[0]
    copy.wait()
    for out, part in ((send, 1 - core), (keep, core)):
        rows = pl.ds(pl.multiple_of(part * size, size), size)
        new = current[rows] - weight * dot3((high[rows], low[rows]), parts)
        out[...] = jnp.where(slot_block[rank] == 0, x[rows], new)


def second_body(flags, slot_block, high, low, *refs):
    blocks, (keep, send, out, x) = refs[:8], refs[8:]
    rank = lax.axis_index("row")
    core, held = bit(rank, 0), slot_block[rank]
    assemble(x, blocks, rank)
    parts = split(x[...])
    weight = flags[0, 1].astype(jnp.float32)
    size = keep.shape[0]
    for current, part in ((keep, core), (send, 1 - core)):
        rows = pl.ds(pl.multiple_of(part * size, size), size)
        new = current[...] - weight * dot3((high[rows], low[rows]), parts)
        out[rows] = jnp.where(held == 0, current[...], jnp.where(held == 1, x[rows], new))


def solve_body(step, inverse, *refs):
    quarters, (out, y) = refs[:4], refs[4:]
    rank = lax.axis_index("row")
    size = quarters[0].shape[0]
    core, z = bit(rank, 0), bit(rank, 1)
    for index, ref in enumerate(quarters):
        place = (core ^ (index >> 1)) * 2 + (z ^ (index & 1))
        y[pl.ds(pl.multiple_of(place * size, size), size)] = ref[...]
    out[...] = dot3(split(inverse[step]), split(y[...]))


def solve(step, inverse, quarters):
    _, rows, depth = inverse.shape
    cols = quarters[0].shape[1]
    vmem = pl.BlockSpec(memory_space=pltpu.VMEM)
    return pl.pallas_call(
        functools.partial(solve_body, step),
        out_shape=jax.ShapeDtypeStruct((rows, cols), jnp.float32),
        in_specs=[vmem] * 5,
        out_specs=vmem,
        scratch_shapes=[pltpu.VMEM((depth, cols), jnp.float32)],
        compiler_params=pltpu.CompilerParams(vmem_limit_bytes=UPDATE_BYTES),
        cost_estimate=pl.CostEstimate(flops=2 * rows * depth * cols, bytes_accessed=4 * rows * cols, transcendentals=0),
        name="solve",
    )(inverse, *quarters)


def update(step, flags, slot_block, pair, blocks, current):
    depth = pair[0].shape[1]
    rows, cols = pair[0].shape[0], blocks[0].shape[1]
    vmem, smem = pl.BlockSpec(memory_space=pltpu.VMEM), pl.BlockSpec(memory_space=pltpu.SMEM)
    counts = (rows // 2, rows // 2) if step == 0 else (rows,)
    scratch = [pltpu.VMEM((depth, cols), jnp.float32)]
    if step == 0:
        scratch += [pltpu.VMEM((rows, cols), jnp.float32), pltpu.SemaphoreType.DMA]
    return pl.pallas_call(
        first_body if step == 0 else second_body,
        out_shape=[jax.ShapeDtypeStruct((count, cols), jnp.float32) for count in counts],
        in_specs=[smem, smem] + [vmem] * 10 + ([pl.BlockSpec(memory_space=pl.ANY)] if step == 0 else [vmem] * 2),
        out_specs=[vmem] * len(counts),
        scratch_shapes=scratch,
        compiler_params=pltpu.CompilerParams(vmem_limit_bytes=UPDATE_BYTES),
        cost_estimate=pl.CostEstimate(flops=6 * rows * depth * cols, bytes_accessed=4 * rows * (depth + 3 * cols), transcendentals=0),
        name="update",
    )(flags, slot_block, *pair, *blocks, *current)


def general(rows, cols, rhs, panel, diag_inverse, flags, slot_block):
    rank = lax.axis_index("row")
    owners = (jnp.argmax(slot_block == 0), jnp.argmax(slot_block == 1))
    weights = flags[0].astype(jnp.float32)
    bits = rows.bit_length() - 1
    current = rhs[0]
    solved = []
    for step in range(2):
        pivot = current
        for b in range(bits - 1):
            pivot = scatter_step(pivot, b, rows, owners[step], rank)
        pivot = cross_step(pivot, bits - 1, rows, owners[step], rank)
        for b in reversed(range(bits - 1)):
            pivot = gather_step(pivot, b, rows, rank)
        x = jnp.dot(diag_inverse[step], pivot, precision=HIGH)
        for b in range(bits):
            x = gather_step(x, b, rows, rank)
        whole = lax.all_gather(panel[0, step], "col", axis=0, tiled=True)
        current = current - weights[step] * jnp.dot(whole, x, precision=HIGH)
        solved.append(x)
    held = slot_block[rank]
    return jnp.where(held == 0, solved[0], jnp.where(held == 1, solved[1], current))[None]


def paced(rows, cols, rhs, panel, diag_inverse, flags, slot_block):
    rank = lax.axis_index("row")
    owner, second = jnp.argmax(slot_block == 0), jnp.argmax(slot_block == 1)
    half = panel.shape[2] // 2
    core = bit(rank, 0)

    def near(one, two):
        return [swap(one, "col", 0, cols), swap(two, "col", 1, cols)]

    def far(one, two):
        return [swap(one, "col", 1, cols), swap(two, "col", 0, cols)]

    def block_halves(panel, step):
        return panel[0, step, :half], panel[0, step, half:]

    def solved(step, y, panel, owner):
        y, panel = tie(y, panel)
        first = near(*block_halves(panel, step))
        y = scatter_step(y, 1, rows, owner, rank)
        y, panel = tie(y, panel)
        top, bottom = block_halves(panel, step)
        second = near(bottom, top)
        y = cross_step(y, 2, rows, owner, rank)
        y, *first = tie(y, *first)
        pieces = far(*first)
        beside = swap(y, "row", 1, rows)
        beside, y, *second = tie(beside, y, *second)
        other, last = swap(y, "row", 0, rows), swap(beside, "row", 0, rows)
        x = solve(step, diag_inverse, [y, beside, other, last])
        x2, x1 = swap(x, "row", 2, rows), swap(x, "row", 1, rows)
        x2, x1, *pieces = tie(x2, x1, *pieces)
        high, low = prepare(panel, step, [*first, *second, *pieces])
        x3 = swap(x2, "row", 1, rows)
        across = [swap(block, "row", 0, rows) for block in (x, x1, x2)]
        x3, high, low, *across = tie(x3, high, low, *across)
        return [x, x1, x2, x3, *across, swap(x3, "row", 0, rows)], (high, low)

    keep, send = halves(rhs[0], core)
    got = swap(send, "row", 0, rows)
    keep, send = tie(keep, send)
    y = jnp.where(bit(owner, 0) == core, keep, got)
    blocks, pair = solved(0, y, panel, owner)
    keep, send = update(0, flags, slot_block, pair, blocks, [rhs])
    got = swap(send, "row", 0, rows)
    y = jnp.where(bit(second, 0) == core, keep, got)
    blocks, pair = solved(1, y, panel, second)
    (result,) = update(1, flags, slot_block, pair, blocks, [keep, send])
    return result[None]


def solution(mesh):
    rows, cols = mesh.shape["row"], mesh.shape["col"]
    form = paced if (rows, cols) == (8, 4) else general

    def shards(*args):
        return form(rows, cols, *args)

    in_specs = (
        P("row", None, "col"),
        P("row", None, "col", None),
        P(None, "row", None),
        P("row", None),
        P(),
    )
    out_specs = P("row", None, "col")
    return jax.shard_map(shards, mesh=mesh, in_specs=in_specs, out_specs=out_specs, check_vma=False)
```

```python
import functools

import jax
import jax.numpy as jnp
from jax import lax
from jax.experimental import pallas as pl
from jax.experimental.pallas import tpu as pltpu
from jax.sharding import PartitionSpec as P

HIGH = lax.Precision.HIGH
PREPARE_BYTES = 4 * 2**20
UPDATE_BYTES = 5 * 2**20


def bit(index, b):
    return (index >> b) & 1


def swap(x, axis, b, size):
    return lax.ppermute(x, axis, [(i, i ^ (1 << b)) for i in range(size)])


def tie(value, *others):
    return lax.optimization_barrier((value, *others))


def join(low_first, a, b):
    return jnp.where(low_first, jnp.concatenate([a, b]), jnp.concatenate([b, a]))


def halves(x, b):
    half = x.shape[0] // 2
    return lax.dynamic_slice_in_dim(x, b * half, half), lax.dynamic_slice_in_dim(x, (1 - b) * half, half)


def scatter_step(x, b, size, owner, me):
    mine = bit(me, b)
    keep, send = halves(x, mine)
    return jnp.where(bit(owner, b) == mine, keep, swap(send, "row", b, size))


def cross_step(x, b, size, owner, me):
    return jnp.where(bit(owner, b) == bit(me, b), x, swap(x, "row", b, size))


def gather_step(x, b, size, me):
    return join(bit(me, b) == 0, x, swap(x, "row", b, size))


def split(x):
    high = x.astype(jnp.bfloat16)
    return high, (x - high.astype(jnp.float32)).astype(jnp.bfloat16)


def dot3(a, b):
    def dot(p, q):
        return jnp.dot(p, q, preferred_element_type=jnp.float32)

    return dot(a[0], b[0]) + (dot(a[0], b[1]) + dot(a[1], b[0]))


def prepare_body(own_top, own_bottom, *refs):
    pieces, (high, low, slots, sems) = refs[:6], refs[6:]
    side = lax.axis_index("col")
    half = pieces[0].shape[0]
    sources = [(own_top, side * 2), (own_bottom, side * 2 + 1)]
    for ref, (distance, part) in zip(pieces, ((1, 0), (2, 1), (1, 1), (2, 0), (3, 0), (3, 1))):
        sources.append((ref, (side ^ distance) * 2 + part))
    groups = [sources[start:start + 2] for start in range(0, 8, 2)]

    def fetch(index):
        copies = []
        start = 0
        for member, (ref, _) in enumerate(groups[index]):
            into = slots.at[index % 2, pl.ds(start, ref.shape[0])]
            copies.append(pltpu.make_async_copy(ref, into, sems.at[index % 2, member]))
            start += ref.shape[0]
        for copy in copies:
            copy.start()
        return copies

    flying = [fetch(0), fetch(1)]
    for index, group in enumerate(groups):
        for copy in flying[index]:
            copy.wait()
        start = 0
        for ref, place in group:
            rows = pl.ds(pl.multiple_of(place * half, half), ref.shape[0])
            high[rows], low[rows] = split(slots[index % 2, pl.ds(start, ref.shape[0])])
            start += ref.shape[0]
        if index + 2 < len(groups):
            flying.append(fetch(index + 2))


def prepare(pieces):
    half, depth = pieces[0].shape
    vmem, anywhere = pl.BlockSpec(memory_space=pltpu.VMEM), pl.BlockSpec(memory_space=pl.ANY)
    return pl.pallas_call(
        prepare_body,
        out_shape=[jax.ShapeDtypeStruct((depth, depth), jnp.bfloat16)] * 2,
        in_specs=[anywhere] * 8,
        out_specs=[vmem] * 2,
        scratch_shapes=[pltpu.VMEM((2, 2 * half, depth), jnp.float32), pltpu.SemaphoreType.DMA((2, 2))],
        compiler_params=pltpu.CompilerParams(vmem_limit_bytes=PREPARE_BYTES),
        cost_estimate=pl.CostEstimate(flops=0, bytes_accessed=16 * depth * depth, transcendentals=0),
        name="prepare",
    )(*pieces)


def assemble(x, blocks, rank):
    core, z = bit(rank, 0), rank >> 1
    share = blocks[0].shape[0]
    for index, ref in enumerate(blocks):
        place = (z ^ (index & 3)) * 2 + (core ^ (index >> 2))
        x[pl.ds(pl.multiple_of(place * share, share), share)] = ref[...]


def first_body(flags, slot_block, high, low, *refs):
    blocks, (rhs, keep, send, x, current, sem) = refs[:8], refs[8:]
    copy = pltpu.make_async_copy(rhs.at[0], current, sem)
    copy.start()
    rank = lax.axis_index("row")
    core = bit(rank, 0)
    assemble(x, blocks, rank)
    parts = split(x[...])
    weight = flags[0, 0].astype(jnp.float32)
    size = keep.shape[0]
    copy.wait()
    for out, part in ((send, 1 - core), (keep, core)):
        rows = pl.ds(pl.multiple_of(part * size, size), size)
        new = current[rows] - weight * dot3((high[rows], low[rows]), parts)
        out[...] = jnp.where(slot_block[rank] == 0, x[rows], new)


def second_body(flags, slot_block, high, low, *refs):
    blocks, (keep, send, out, x) = refs[:8], refs[8:]
    rank = lax.axis_index("row")
    core, held = bit(rank, 0), slot_block[rank]
    assemble(x, blocks, rank)
    parts = split(x[...])
    weight = flags[0, 1].astype(jnp.float32)
    size = keep.shape[0]
    for current, part in ((keep, core), (send, 1 - core)):
        rows = pl.ds(pl.multiple_of(part * size, size), size)
        new = current[...] - weight * dot3((high[rows], low[rows]), parts)
        out[rows] = jnp.where(held == 0, current[...], jnp.where(held == 1, x[rows], new))


def solve_body(inverse, *refs):
    quarters, (out, y) = refs[:4], refs[4:]
    rank = lax.axis_index("row")
    size = quarters[0].shape[0]
    core, z = bit(rank, 0), bit(rank, 1)
    for index, ref in enumerate(quarters):
        place = (core ^ (index >> 1)) * 2 + (z ^ (index & 1))
        y[pl.ds(pl.multiple_of(place * size, size), size)] = ref[...]
    out[...] = dot3(split(inverse[...]), split(y[...]))


def solve(inverse, quarters):
    rows, depth = inverse.shape
    cols = quarters[0].shape[1]
    vmem = pl.BlockSpec(memory_space=pltpu.VMEM)
    return pl.pallas_call(
        solve_body,
        out_shape=jax.ShapeDtypeStruct((rows, cols), jnp.float32),
        in_specs=[vmem] * 5,
        out_specs=vmem,
        scratch_shapes=[pltpu.VMEM((depth, cols), jnp.float32)],
        compiler_params=pltpu.CompilerParams(vmem_limit_bytes=UPDATE_BYTES),
        cost_estimate=pl.CostEstimate(flops=2 * rows * depth * cols, bytes_accessed=4 * rows * cols, transcendentals=0),
        name="solve",
    )(inverse, *quarters)


def update(step, flags, slot_block, pair, blocks, current):
    depth = pair[0].shape[1]
    rows, cols = pair[0].shape[0], blocks[0].shape[1]
    vmem, smem = pl.BlockSpec(memory_space=pltpu.VMEM), pl.BlockSpec(memory_space=pltpu.SMEM)
    counts = (rows // 2, rows // 2) if step == 0 else (rows,)
    scratch = [pltpu.VMEM((depth, cols), jnp.float32)]
    if step == 0:
        scratch += [pltpu.VMEM((rows, cols), jnp.float32), pltpu.SemaphoreType.DMA]
    return pl.pallas_call(
        first_body if step == 0 else second_body,
        out_shape=[jax.ShapeDtypeStruct((count, cols), jnp.float32) for count in counts],
        in_specs=[smem, smem] + [vmem] * 10 + ([pl.BlockSpec(memory_space=pl.ANY)] if step == 0 else [vmem] * 2),
        out_specs=[vmem] * len(counts),
        scratch_shapes=scratch,
        compiler_params=pltpu.CompilerParams(vmem_limit_bytes=UPDATE_BYTES),
        cost_estimate=pl.CostEstimate(flops=6 * rows * depth * cols, bytes_accessed=4 * rows * (depth + 3 * cols), transcendentals=0),
        name="update",
    )(flags, slot_block, *pair, *blocks, *current)


def general(rows, cols, rhs, panel, diag_inverse, flags, slot_block):
    rank = lax.axis_index("row")
    owners = (jnp.argmax(slot_block == 0), jnp.argmax(slot_block == 1))
    weights = flags[0].astype(jnp.float32)
    bits = rows.bit_length() - 1
    current = rhs[0]
    solved = []
    for step in range(2):
        pivot = current
        for b in range(bits - 1):
            pivot = scatter_step(pivot, b, rows, owners[step], rank)
        pivot = cross_step(pivot, bits - 1, rows, owners[step], rank)
        for b in reversed(range(bits - 1)):
            pivot = gather_step(pivot, b, rows, rank)
        x = jnp.dot(diag_inverse[step], pivot, precision=HIGH)
        for b in range(bits):
            x = gather_step(x, b, rows, rank)
        whole = lax.all_gather(panel[0, step], "col", axis=0, tiled=True)
        current = current - weights[step] * jnp.dot(whole, x, precision=HIGH)
        solved.append(x)
    held = slot_block[rank]
    return jnp.where(held == 0, solved[0], jnp.where(held == 1, solved[1], current))[None]


def paced(rows, cols, rhs, panel, diag_inverse, flags, slot_block):
    rank = lax.axis_index("row")
    owner, second = jnp.argmax(slot_block == 0), jnp.argmax(slot_block == 1)
    half = panel.shape[2] // 2
    core = bit(rank, 0)

    def near(one, two):
        return [swap(one, "col", 0, cols), swap(two, "col", 1, cols)]

    def far(one, two):
        return [swap(one, "col", 1, cols), swap(two, "col", 0, cols)]

    def block_halves(panel, step):
        return panel[0, step, :half], panel[0, step, half:]

    def solved(step, y, panel, owner):
        y, panel = tie(y, panel)
        block = tie(*block_halves(panel, step))
        first = near(*block)
        y = scatter_step(y, 1, rows, owner, rank)
        y, *block = tie(y, *block)
        second = near(*block[::-1])
        y = cross_step(y, 2, rows, owner, rank)
        y, inverse, *first = tie(y, diag_inverse, *first)
        pieces = far(*first)
        beside = swap(y, "row", 1, rows)
        beside, y, *second = tie(beside, y, *second)
        other, last = swap(y, "row", 0, rows), swap(beside, "row", 0, rows)
        x = solve(inverse[step], [y, beside, other, last])
        x2, x1 = swap(x, "row", 2, rows), swap(x, "row", 1, rows)
        x2, x1, *pieces = tie(x2, x1, *pieces)
        high, low = prepare([*block, *first, *second, *pieces])
        x3 = swap(x2, "row", 1, rows)
        across = [swap(block, "row", 0, rows) for block in (x, x1, x2)]
        x3, high, low, *across = tie(x3, high, low, *across)
        return [x, x1, x2, x3, *across, swap(x3, "row", 0, rows)], (high, low)

    keep, send = halves(rhs[0], core)
    got = swap(send, "row", 0, rows)
    keep, send = tie(keep, send)
    y = jnp.where(bit(owner, 0) == core, keep, got)
    blocks, pair = solved(0, y, panel, owner)
    keep, send = update(0, flags, slot_block, pair, blocks, [rhs])
    got = swap(send, "row", 0, rows)
    y = jnp.where(bit(second, 0) == core, keep, got)
    blocks, pair = solved(1, y, panel, second)
    (result,) = update(1, flags, slot_block, pair, blocks, [keep, send])
    return result[None]


def solution(mesh):
    rows, cols = mesh.shape["row"], mesh.shape["col"]
    form = paced if (rows, cols) == (8, 4) else general

    def shards(*args):
        return form(rows, cols, *args)

    in_specs = (
        P("row", None, "col"),
        P("row", None, "col", None),
        P(None, "row", None),
        P("row", None),
        P(),
    )
    out_specs = P("row", None, "col")
    return jax.shard_map(shards, mesh=mesh, in_specs=in_specs, out_specs=out_specs, check_vma=False)
```

```python
import functools

import jax
import jax.numpy as jnp
from jax import lax
from jax.experimental import pallas as pl
from jax.experimental.pallas import tpu as pltpu
from jax.sharding import PartitionSpec as P

HIGH = lax.Precision.HIGH
PREPARE_BYTES = 4 * 2**20
UPDATE_BYTES = 5 * 2**20


def bit(index, b):
    return (index >> b) & 1


def swap(x, axis, b, size):
    return lax.ppermute(x, axis, [(i, i ^ (1 << b)) for i in range(size)])


def tie(value, *others):
    return lax.optimization_barrier((value, *others))


def join(low_first, a, b):
    return jnp.where(low_first, jnp.concatenate([a, b]), jnp.concatenate([b, a]))


def halves(x, b):
    half = x.shape[0] // 2
    return lax.dynamic_slice_in_dim(x, b * half, half), lax.dynamic_slice_in_dim(x, (1 - b) * half, half)


def scatter_step(x, b, size, owner, me):
    mine = bit(me, b)
    keep, send = halves(x, mine)
    return jnp.where(bit(owner, b) == mine, keep, swap(send, "row", b, size))


def cross_step(x, b, size, owner, me):
    return jnp.where(bit(owner, b) == bit(me, b), x, swap(x, "row", b, size))


def gather_step(x, b, size, me):
    return join(bit(me, b) == 0, x, swap(x, "row", b, size))


def split(x):
    high = x.astype(jnp.bfloat16)
    return high, (x - high.astype(jnp.float32)).astype(jnp.bfloat16)


def dot3(a, b):
    def dot(p, q):
        return jnp.dot(p, q, preferred_element_type=jnp.float32)

    return dot(a[0], b[0]) + (dot(a[0], b[1]) + dot(a[1], b[0]))


def prepare_body(own_top, own_bottom, *refs):
    pieces, (high, low, slots, sems) = refs[:6], refs[6:]
    side = lax.axis_index("col")
    half = pieces[0].shape[0]
    sources = [(own_top, side * 2), (own_bottom, side * 2 + 1)]
    for ref, (distance, part) in zip(pieces, ((1, 0), (2, 1), (1, 1), (2, 0), (3, 0), (3, 1))):
        sources.append((ref, (side ^ distance) * 2 + part))
    groups = [sources[start:start + 2] for start in range(0, 8, 2)]

    def fetch(index):
        copies = []
        start = 0
        for member, (ref, _) in enumerate(groups[index]):
            into = slots.at[index % 2, pl.ds(start, ref.shape[0])]
            copies.append(pltpu.make_async_copy(ref, into, sems.at[index % 2, member]))
            start += ref.shape[0]
        for copy in copies:
            copy.start()
        return copies

    flying = [fetch(0), fetch(1)]
    for index, group in enumerate(groups):
        for copy in flying[index]:
            copy.wait()
        start = 0
        for ref, place in group:
            rows = pl.ds(pl.multiple_of(place * half, half), ref.shape[0])
            high[rows], low[rows] = split(slots[index % 2, pl.ds(start, ref.shape[0])])
            start += ref.shape[0]
        if index + 2 < len(groups):
            flying.append(fetch(index + 2))


def prepare(pieces):
    half, depth = pieces[0].shape
    vmem, anywhere = pl.BlockSpec(memory_space=pltpu.VMEM), pl.BlockSpec(memory_space=pl.ANY)
    return pl.pallas_call(
        prepare_body,
        out_shape=[jax.ShapeDtypeStruct((depth, depth), jnp.bfloat16)] * 2,
        in_specs=[anywhere] * 8,
        out_specs=[vmem] * 2,
        scratch_shapes=[pltpu.VMEM((2, 2 * half, depth), jnp.float32), pltpu.SemaphoreType.DMA((2, 2))],
        compiler_params=pltpu.CompilerParams(vmem_limit_bytes=PREPARE_BYTES),
        cost_estimate=pl.CostEstimate(flops=0, bytes_accessed=16 * depth * depth, transcendentals=0),
        name="prepare",
    )(*pieces)


def assemble(x, blocks, rank):
    core, z = bit(rank, 0), rank >> 1
    share = blocks[0].shape[0]
    for index, ref in enumerate(blocks):
        place = (z ^ (index & 3)) * 2 + (core ^ (index >> 2))
        x[pl.ds(pl.multiple_of(place * share, share), share)] = ref[...]


def first_body(flags, slot_block, high, low, *refs):
    blocks, (rhs, keep, send, x, current, sem) = refs[:8], refs[8:]
    copy = pltpu.make_async_copy(rhs.at[0], current, sem)
    copy.start()
    rank = lax.axis_index("row")
    core = bit(rank, 0)
    assemble(x, blocks, rank)
    parts = split(x[...])
    weight = flags[0, 0].astype(jnp.float32)
    size = keep.shape[0]
    copy.wait()
    for out, part in ((send, 1 - core), (keep, core)):
        rows = pl.ds(pl.multiple_of(part * size, size), size)
        new = current[rows] - weight * dot3((high[rows], low[rows]), parts)
        out[...] = jnp.where(slot_block[rank] == 0, x[rows], new)


def second_body(flags, slot_block, high, low, *refs):
    blocks, (keep, send, out, x) = refs[:8], refs[8:]
    rank = lax.axis_index("row")
    core, held = bit(rank, 0), slot_block[rank]
    assemble(x, blocks, rank)
    parts = split(x[...])
    weight = flags[0, 1].astype(jnp.float32)
    size = keep.shape[0]
    for current, part in ((keep, core), (send, 1 - core)):
        rows = pl.ds(pl.multiple_of(part * size, size), size)
        new = current[...] - weight * dot3((high[rows], low[rows]), parts)
        out[rows] = jnp.where(held == 0, current[...], jnp.where(held == 1, x[rows], new))


def solve_body(inverse, *refs):
    chunks, (out, y) = refs[:8], refs[8:]
    rank = lax.axis_index("row")
    size = chunks[0].shape[0]
    core, z = bit(rank, 0), bit(rank, 1)
    for index, ref in enumerate(chunks):
        quarter = (core ^ (index >> 2)) * 2 + (z ^ ((index >> 1) & 1))
        place = quarter * 2 + (index & 1)
        y[pl.ds(pl.multiple_of(place * size, size), size)] = ref[...]
    out[...] = dot3(split(inverse[...]), split(y[...]))


def solve(inverse, chunks):
    rows, depth = inverse.shape
    cols = chunks[0].shape[1]
    vmem = pl.BlockSpec(memory_space=pltpu.VMEM)
    return pl.pallas_call(
        solve_body,
        out_shape=jax.ShapeDtypeStruct((rows, cols), jnp.float32),
        in_specs=[vmem] * 9,
        out_specs=vmem,
        scratch_shapes=[pltpu.VMEM((depth, cols), jnp.float32)],
        compiler_params=pltpu.CompilerParams(vmem_limit_bytes=UPDATE_BYTES),
        cost_estimate=pl.CostEstimate(flops=2 * rows * depth * cols, bytes_accessed=4 * rows * cols, transcendentals=0),
        name="solve",
    )(inverse, *chunks)


def update(step, flags, slot_block, pair, blocks, current):
    depth = pair[0].shape[1]
    rows, cols = pair[0].shape[0], blocks[0].shape[1]
    vmem, smem = pl.BlockSpec(memory_space=pltpu.VMEM), pl.BlockSpec(memory_space=pltpu.SMEM)
    counts = (rows // 2, rows // 2) if step == 0 else (rows,)
    scratch = [pltpu.VMEM((depth, cols), jnp.float32)]
    if step == 0:
        scratch += [pltpu.VMEM((rows, cols), jnp.float32), pltpu.SemaphoreType.DMA]
    return pl.pallas_call(
        first_body if step == 0 else second_body,
        out_shape=[jax.ShapeDtypeStruct((count, cols), jnp.float32) for count in counts],
        in_specs=[smem, smem] + [vmem] * 10 + ([pl.BlockSpec(memory_space=pl.ANY)] if step == 0 else [vmem] * 2),
        out_specs=[vmem] * len(counts),
        scratch_shapes=scratch,
        compiler_params=pltpu.CompilerParams(vmem_limit_bytes=UPDATE_BYTES),
        cost_estimate=pl.CostEstimate(flops=6 * rows * depth * cols, bytes_accessed=4 * rows * (depth + 3 * cols), transcendentals=0),
        name="update",
    )(flags, slot_block, *pair, *blocks, *current)


def general(rows, cols, rhs, panel, diag_inverse, flags, slot_block):
    rank = lax.axis_index("row")
    owners = (jnp.argmax(slot_block == 0), jnp.argmax(slot_block == 1))
    weights = flags[0].astype(jnp.float32)
    bits = rows.bit_length() - 1
    current = rhs[0]
    solved = []
    for step in range(2):
        pivot = current
        for b in range(bits - 1):
            pivot = scatter_step(pivot, b, rows, owners[step], rank)
        pivot = cross_step(pivot, bits - 1, rows, owners[step], rank)
        for b in reversed(range(bits - 1)):
            pivot = gather_step(pivot, b, rows, rank)
        x = jnp.dot(diag_inverse[step], pivot, precision=HIGH)
        for b in range(bits):
            x = gather_step(x, b, rows, rank)
        whole = lax.all_gather(panel[0, step], "col", axis=0, tiled=True)
        current = current - weights[step] * jnp.dot(whole, x, precision=HIGH)
        solved.append(x)
    held = slot_block[rank]
    return jnp.where(held == 0, solved[0], jnp.where(held == 1, solved[1], current))[None]


def paced(rows, cols, rhs, panel, diag_inverse, flags, slot_block):
    rank = lax.axis_index("row")
    owner, second = jnp.argmax(slot_block == 0), jnp.argmax(slot_block == 1)
    half = panel.shape[2] // 2
    core = bit(rank, 0)

    def near(one, two):
        return [swap(one, "col", 0, cols), swap(two, "col", 1, cols)]

    def far(one, two):
        return [swap(one, "col", 1, cols), swap(two, "col", 0, cols)]

    def block_halves(panel, step):
        return panel[0, step, :half], panel[0, step, half:]

    def solved(step, y, panel, owner):
        y, panel = tie(y, panel)
        block = tie(*block_halves(panel, step))
        first = near(*block)
        keep, send = halves(y, bit(rank, 1))
        size = keep.shape[0] // 2
        parts = tie(*[half[start:start + size] for half in (send, keep) for start in (0, size)])
        own = []
        for send, keep in zip(parts[:2], parts[2:]):
            own.append(jnp.where(bit(owner, 1) == bit(rank, 1), keep, swap(send, "row", 1, rows)))
        own[1], *block = tie(own[1], *block)
        second = near(*block[::-1])
        own = [cross_step(chunk, 2, rows, owner, rank) for chunk in own]
        own[1], *first = tie(own[1], *first)
        pieces = far(*first)
        own[0], inverse = tie(own[0], diag_inverse)
        beside = [swap(chunk, "row", 1, rows) for chunk in own]
        *chunks, second[0], second[1] = tie(*own, *beside, *second)
        x = solve(inverse[step], chunks + [swap(chunk, "row", 0, rows) for chunk in chunks])
        x2, x1 = swap(x, "row", 2, rows), swap(x, "row", 1, rows)
        x2, x1, *pieces = tie(x2, x1, *pieces)
        high, low = prepare([*block, *first, *second, *pieces])
        x3 = swap(x2, "row", 1, rows)
        across = [swap(block, "row", 0, rows) for block in (x, x1, x2)]
        x3, high, low, *across = tie(x3, high, low, *across)
        return [x, x1, x2, x3, *across, swap(x3, "row", 0, rows)], (high, low)

    keep, send = halves(rhs[0], core)
    got = swap(send, "row", 0, rows)
    keep, send = tie(keep, send)
    y = jnp.where(bit(owner, 0) == core, keep, got)
    blocks, pair = solved(0, y, panel, owner)
    keep, send = update(0, flags, slot_block, pair, blocks, [rhs])
    got = swap(send, "row", 0, rows)
    y = jnp.where(bit(second, 0) == core, keep, got)
    blocks, pair = solved(1, y, panel, second)
    (result,) = update(1, flags, slot_block, pair, blocks, [keep, send])
    return result[None]


def solution(mesh):
    rows, cols = mesh.shape["row"], mesh.shape["col"]
    form = paced if (rows, cols) == (8, 4) else general

    def shards(*args):
        return form(rows, cols, *args)

    in_specs = (
        P("row", None, "col"),
        P("row", None, "col", None),
        P(None, "row", None),
        P("row", None),
        P(),
    )
    out_specs = P("row", None, "col")
    return jax.shard_map(shards, mesh=mesh, in_specs=in_specs, out_specs=out_specs, check_vma=False)
```

```python
import functools

import jax
import jax.numpy as jnp
from jax import lax
from jax.experimental import pallas as pl
from jax.experimental.pallas import tpu as pltpu
from jax.sharding import PartitionSpec as P

HIGH = lax.Precision.HIGH
PREPARE_BYTES = 4 * 2**20
UPDATE_BYTES = 5 * 2**20


def bit(index, b):
    return (index >> b) & 1


def swap(x, axis, b, size):
    return lax.ppermute(x, axis, [(i, i ^ (1 << b)) for i in range(size)])


def tie(value, *others):
    return lax.optimization_barrier((value, *others))


def join(low_first, a, b):
    return jnp.where(low_first, jnp.concatenate([a, b]), jnp.concatenate([b, a]))


def halves(x, b):
    half = x.shape[0] // 2
    return lax.dynamic_slice_in_dim(x, b * half, half), lax.dynamic_slice_in_dim(x, (1 - b) * half, half)


def scatter_step(x, b, size, owner, me):
    mine = bit(me, b)
    keep, send = halves(x, mine)
    return jnp.where(bit(owner, b) == mine, keep, swap(send, "row", b, size))


def cross_step(x, b, size, owner, me):
    return jnp.where(bit(owner, b) == bit(me, b), x, swap(x, "row", b, size))


def gather_step(x, b, size, me):
    return join(bit(me, b) == 0, x, swap(x, "row", b, size))


def split(x):
    high = x.astype(jnp.bfloat16)
    return high, (x - high.astype(jnp.float32)).astype(jnp.bfloat16)


def dot3(a, b):
    def dot(p, q):
        return jnp.dot(p, q, preferred_element_type=jnp.float32)

    return dot(a[0], b[0]) + (dot(a[0], b[1]) + dot(a[1], b[0]))


def prepare_body(own_top, own_bottom, *refs):
    pieces, (high, low, slots, sems) = refs[:6], refs[6:]
    side = lax.axis_index("col")
    half = pieces[0].shape[0]
    sources = [(own_top, side * 2), (own_bottom, side * 2 + 1)]
    for ref, (distance, part) in zip(pieces, ((1, 0), (2, 1), (1, 1), (2, 0), (3, 0), (3, 1))):
        sources.append((ref, (side ^ distance) * 2 + part))
    groups = [sources[start:start + 2] for start in range(0, 8, 2)]

    def fetch(index):
        copies = []
        start = 0
        for member, (ref, _) in enumerate(groups[index]):
            into = slots.at[index % 2, pl.ds(start, ref.shape[0])]
            copies.append(pltpu.make_async_copy(ref, into, sems.at[index % 2, member]))
            start += ref.shape[0]
        for copy in copies:
            copy.start()
        return copies

    flying = [fetch(0), fetch(1)]
    for index, group in enumerate(groups):
        for copy in flying[index]:
            copy.wait()
        start = 0
        for ref, place in group:
            rows = pl.ds(pl.multiple_of(place * half, half), ref.shape[0])
            high[rows], low[rows] = split(slots[index % 2, pl.ds(start, ref.shape[0])])
            start += ref.shape[0]
        if index + 2 < len(groups):
            flying.append(fetch(index + 2))


def prepare(pieces):
    half, depth = pieces[0].shape
    vmem, anywhere = pl.BlockSpec(memory_space=pltpu.VMEM), pl.BlockSpec(memory_space=pl.ANY)
    return pl.pallas_call(
        prepare_body,
        out_shape=[jax.ShapeDtypeStruct((depth, depth), jnp.bfloat16)] * 2,
        in_specs=[anywhere] * 8,
        out_specs=[vmem] * 2,
        scratch_shapes=[pltpu.VMEM((2, 2 * half, depth), jnp.float32), pltpu.SemaphoreType.DMA((2, 2))],
        compiler_params=pltpu.CompilerParams(vmem_limit_bytes=PREPARE_BYTES),
        cost_estimate=pl.CostEstimate(flops=0, bytes_accessed=16 * depth * depth, transcendentals=0),
        name="prepare",
    )(*pieces)


def assemble(x, blocks, rank):
    core, z = bit(rank, 0), rank >> 1
    share = blocks[0].shape[0]
    for index, ref in enumerate(blocks):
        place = (z ^ (index & 3)) * 2 + (core ^ (index >> 2))
        x[pl.ds(pl.multiple_of(place * share, share), share)] = ref[...]


def first_body(flags, slot_block, high, low, *refs):
    blocks, (rhs, keep, send, x, current, sem) = refs[:8], refs[8:]
    copy = pltpu.make_async_copy(rhs.at[0], current, sem)
    copy.start()
    rank = lax.axis_index("row")
    core = bit(rank, 0)
    assemble(x, blocks, rank)
    parts = split(x[...])
    weight = flags[0, 0].astype(jnp.float32)
    size = keep.shape[0]
    copy.wait()
    for out, part in ((send, 1 - core), (keep, core)):
        rows = pl.ds(pl.multiple_of(part * size, size), size)
        new = current[rows] - weight * dot3((high[rows], low[rows]), parts)
        out[...] = jnp.where(slot_block[rank] == 0, x[rows], new)


def second_body(flags, slot_block, high, low, *refs):
    blocks, (keep, send, out, x, rows_out, sems) = refs[:8], refs[8:]
    rank = lax.axis_index("row")
    core, held = bit(rank, 0), slot_block[rank]
    assemble(x, blocks, rank)
    parts = split(x[...])
    weight = flags[0, 1].astype(jnp.float32)
    size = keep.shape[0]
    copies = []
    for index, (current, part) in enumerate(((keep, core), (send, 1 - core))):
        rows = pl.ds(pl.multiple_of(part * size, size), size)
        new = current[...] - weight * dot3((high[rows], low[rows]), parts)
        rows_out[index] = jnp.where(held == 0, current[...], jnp.where(held == 1, x[rows], new))
        copies.append(pltpu.make_async_copy(rows_out.at[index], out.at[rows], sems.at[index]))
        copies[index].start()
    for copy in copies:
        copy.wait()


def solve_body(inverse, *refs):
    quarters, (out, y) = refs[:4], refs[4:]
    rank = lax.axis_index("row")
    size = quarters[0].shape[0]
    core, z = bit(rank, 0), bit(rank, 1)
    for index, ref in enumerate(quarters):
        place = (core ^ (index >> 1)) * 2 + (z ^ (index & 1))
        y[pl.ds(pl.multiple_of(place * size, size), size)] = ref[...]
    out[...] = dot3(split(inverse[...]), split(y[...]))


def solve(inverse, quarters):
    rows, depth = inverse.shape
    cols = quarters[0].shape[1]
    vmem = pl.BlockSpec(memory_space=pltpu.VMEM)
    return pl.pallas_call(
        solve_body,
        out_shape=jax.ShapeDtypeStruct((rows, cols), jnp.float32),
        in_specs=[vmem] * 5,
        out_specs=vmem,
        scratch_shapes=[pltpu.VMEM((depth, cols), jnp.float32)],
        compiler_params=pltpu.CompilerParams(vmem_limit_bytes=UPDATE_BYTES),
        cost_estimate=pl.CostEstimate(flops=2 * rows * depth * cols, bytes_accessed=4 * rows * cols, transcendentals=0),
        name="solve",
    )(inverse, *quarters)


def update(step, flags, slot_block, pair, blocks, current):
    depth = pair[0].shape[1]
    rows, cols = pair[0].shape[0], blocks[0].shape[1]
    vmem, smem = pl.BlockSpec(memory_space=pltpu.VMEM), pl.BlockSpec(memory_space=pltpu.SMEM)
    counts = (rows // 2, rows // 2) if step == 0 else (rows,)
    scratch = [pltpu.VMEM((depth, cols), jnp.float32)]
    if step == 0:
        scratch += [pltpu.VMEM((rows, cols), jnp.float32), pltpu.SemaphoreType.DMA]
    else:
        scratch += [pltpu.VMEM((2, rows // 2, cols), jnp.float32), pltpu.SemaphoreType.DMA((2,))]
    return pl.pallas_call(
        first_body if step == 0 else second_body,
        out_shape=[jax.ShapeDtypeStruct((count, cols), jnp.float32) for count in counts],
        in_specs=[smem, smem] + [vmem] * 10 + ([pl.BlockSpec(memory_space=pl.ANY)] if step == 0 else [vmem] * 2),
        out_specs=[vmem] * 2 if step == 0 else [pl.BlockSpec(memory_space=pl.ANY)],
        scratch_shapes=scratch,
        compiler_params=pltpu.CompilerParams(vmem_limit_bytes=UPDATE_BYTES),
        cost_estimate=pl.CostEstimate(flops=6 * rows * depth * cols, bytes_accessed=4 * rows * (depth + 3 * cols), transcendentals=0),
        name="update",
    )(flags, slot_block, *pair, *blocks, *current)


def general(rows, cols, rhs, panel, diag_inverse, flags, slot_block):
    rank = lax.axis_index("row")
    owners = (jnp.argmax(slot_block == 0), jnp.argmax(slot_block == 1))
    weights = flags[0].astype(jnp.float32)
    bits = rows.bit_length() - 1
    current = rhs[0]
    solved = []
    for step in range(2):
        pivot = current
        for b in range(bits - 1):
            pivot = scatter_step(pivot, b, rows, owners[step], rank)
        pivot = cross_step(pivot, bits - 1, rows, owners[step], rank)
        for b in reversed(range(bits - 1)):
            pivot = gather_step(pivot, b, rows, rank)
        x = jnp.dot(diag_inverse[step], pivot, precision=HIGH)
        for b in range(bits):
            x = gather_step(x, b, rows, rank)
        whole = lax.all_gather(panel[0, step], "col", axis=0, tiled=True)
        current = current - weights[step] * jnp.dot(whole, x, precision=HIGH)
        solved.append(x)
    held = slot_block[rank]
    return jnp.where(held == 0, solved[0], jnp.where(held == 1, solved[1], current))[None]


def paced(rows, cols, rhs, panel, diag_inverse, flags, slot_block):
    rank = lax.axis_index("row")
    owner, second = jnp.argmax(slot_block == 0), jnp.argmax(slot_block == 1)
    half = panel.shape[2] // 2
    core = bit(rank, 0)

    def near(one, two):
        return [swap(one, "col", 0, cols), swap(two, "col", 1, cols)]

    def far(one, two):
        return [swap(one, "col", 1, cols), swap(two, "col", 0, cols)]

    def block_halves(panel, step):
        return panel[0, step, :half], panel[0, step, half:]

    def solved(step, y, panel, owner):
        y, panel = tie(y, panel)
        block = tie(*block_halves(panel, step))
        first = near(*block)
        y = scatter_step(y, 1, rows, owner, rank)
        y, *block = tie(y, *block)
        second = near(*block[::-1])
        y = cross_step(y, 2, rows, owner, rank)
        y, inverse, *first = tie(y, diag_inverse, *first)
        pieces = far(*first)
        beside = swap(y, "row", 1, rows)
        y, *second = tie(y, *second)
        other = swap(y, "row", 0, rows)
        beside, inverse = tie(beside, inverse[step])
        last = swap(beside, "row", 0, rows)
        x = solve(inverse, [y, beside, other, last])
        x2, x1 = swap(x, "row", 2, rows), swap(x, "row", 1, rows)
        x2, x1, *pieces = tie(x2, x1, *pieces)
        high, low = prepare([*block, *first, *second, *pieces])
        x3 = swap(x2, "row", 1, rows)
        across = [swap(block, "row", 0, rows) for block in (x, x1, x2)]
        x3, high, low, *across = tie(x3, high, low, *across)
        return [x, x1, x2, x3, *across, swap(x3, "row", 0, rows)], (high, low)

    got = swap(halves(rhs[0], 1 - core)[0], "row", 0, rows)
    kept, owner = tie(rhs, owner)
    keep, owner = tie(halves(kept[0], core)[0], owner)
    y = jnp.where(bit(owner, 0) == core, keep, got)
    blocks, pair = solved(0, y, panel, owner)
    keep, send = update(0, flags, slot_block, pair, blocks, [rhs])
    got = swap(send, "row", 0, rows)
    y = jnp.where(bit(second, 0) == core, keep, got)
    blocks, pair = solved(1, y, panel, second)
    (result,) = update(1, flags, slot_block, pair, blocks, [keep, send])
    return result[None]


def solution(mesh):
    rows, cols = mesh.shape["row"], mesh.shape["col"]
    form = paced if (rows, cols) == (8, 4) else general

    def shards(*args):
        return form(rows, cols, *args)

    in_specs = (
        P("row", None, "col"),
        P("row", None, "col", None),
        P(None, "row", None),
        P("row", None),
        P(),
    )
    out_specs = P("row", None, "col")
    return jax.shard_map(shards, mesh=mesh, in_specs=in_specs, out_specs=out_specs, check_vma=False)
```

```python
import functools

import jax
import jax.numpy as jnp
from jax import lax
from jax.experimental import pallas as pl
from jax.experimental.pallas import tpu as pltpu
from jax.sharding import PartitionSpec as P

HIGH = lax.Precision.HIGH
PREPARE_BYTES = 4 * 2**20
UPDATE_BYTES = 5 * 2**20


def bit(index, b):
    return (index >> b) & 1


def swap(x, axis, b, size):
    return lax.ppermute(x, axis, [(i, i ^ (1 << b)) for i in range(size)])


def tie(value, *others):
    return lax.optimization_barrier((value, *others))


def join(low_first, a, b):
    return jnp.where(low_first, jnp.concatenate([a, b]), jnp.concatenate([b, a]))


def halves(x, b):
    half = x.shape[0] // 2
    return lax.dynamic_slice_in_dim(x, b * half, half), lax.dynamic_slice_in_dim(x, (1 - b) * half, half)


def scatter_step(x, b, size, owner, me):
    mine = bit(me, b)
    keep, send = halves(x, mine)
    return jnp.where(bit(owner, b) == mine, keep, swap(send, "row", b, size))


def cross_step(x, b, size, owner, me):
    return jnp.where(bit(owner, b) == bit(me, b), x, swap(x, "row", b, size))


def gather_step(x, b, size, me):
    return join(bit(me, b) == 0, x, swap(x, "row", b, size))


def split(x):
    high = x.astype(jnp.bfloat16)
    return high, (x - high.astype(jnp.float32)).astype(jnp.bfloat16)


def dot3(a, b):
    def dot(p, q):
        return jnp.dot(p, q, preferred_element_type=jnp.float32)

    return dot(a[0], b[0]) + (dot(a[0], b[1]) + dot(a[1], b[0]))


def prepare_body(own_top, own_bottom, *refs):
    pieces, (high, low, slots, sems) = refs[:6], refs[6:]
    side = lax.axis_index("col")
    half = pieces[0].shape[0]
    sources = [(own_top, side * 2), (own_bottom, side * 2 + 1)]
    for ref, (distance, part) in zip(pieces, ((1, 0), (2, 1), (1, 1), (2, 0), (3, 0), (3, 1))):
        sources.append((ref, (side ^ distance) * 2 + part))
    groups = [sources[start:start + 2] for start in range(0, 8, 2)]

    def fetch(index):
        copies = []
        start = 0
        for member, (ref, _) in enumerate(groups[index]):
            into = slots.at[index % 2, pl.ds(start, ref.shape[0])]
            copies.append(pltpu.make_async_copy(ref, into, sems.at[index % 2, member]))
            start += ref.shape[0]
        for copy in copies:
            copy.start()
        return copies

    flying = [fetch(0), fetch(1)]
    for index, group in enumerate(groups):
        for copy in flying[index]:
            copy.wait()
        start = 0
        for ref, place in group:
            rows = pl.ds(pl.multiple_of(place * half, half), ref.shape[0])
            high[rows], low[rows] = split(slots[index % 2, pl.ds(start, ref.shape[0])])
            start += ref.shape[0]
        if index + 2 < len(groups):
            flying.append(fetch(index + 2))


def prepare(pieces):
    half, depth = pieces[0].shape
    vmem, anywhere = pl.BlockSpec(memory_space=pltpu.VMEM), pl.BlockSpec(memory_space=pl.ANY)
    return pl.pallas_call(
        prepare_body,
        out_shape=[jax.ShapeDtypeStruct((depth, depth), jnp.bfloat16)] * 2,
        in_specs=[anywhere] * 8,
        out_specs=[vmem] * 2,
        scratch_shapes=[pltpu.VMEM((2, 2 * half, depth), jnp.float32), pltpu.SemaphoreType.DMA((2, 2))],
        compiler_params=pltpu.CompilerParams(vmem_limit_bytes=PREPARE_BYTES),
        cost_estimate=pl.CostEstimate(flops=0, bytes_accessed=16 * depth * depth, transcendentals=0),
        name="prepare",
    )(*pieces)


def cut_body(block, send, keep, sems):
    core = bit(lax.axis_index("row"), 0)
    size = send.shape[0]
    copies = []
    for index, (out, part) in enumerate(((send, 1 - core), (keep, core))):
        rows = pl.ds(pl.multiple_of(part * size, size), size)
        copies.append(pltpu.make_async_copy(block.at[0, rows], out, sems.at[index]))
        copies[index].start()
    for copy in copies:
        copy.wait()


def cut(block):
    _, rows, cols = block.shape
    return pl.pallas_call(
        cut_body,
        out_shape=[jax.ShapeDtypeStruct((rows // 2, cols), jnp.float32)] * 2,
        in_specs=[pl.BlockSpec(memory_space=pl.ANY)],
        out_specs=[pl.BlockSpec(memory_space=pltpu.VMEM)] * 2,
        scratch_shapes=[pltpu.SemaphoreType.DMA((2,))],
        compiler_params=pltpu.CompilerParams(vmem_limit_bytes=PREPARE_BYTES),
        cost_estimate=pl.CostEstimate(flops=0, bytes_accessed=8 * rows * cols, transcendentals=0),
        name="cut",
    )(block)


def assemble(x, blocks, rank):
    core, z = bit(rank, 0), rank >> 1
    share = blocks[0].shape[0]
    for index, ref in enumerate(blocks):
        place = (z ^ (index & 3)) * 2 + (core ^ (index >> 2))
        x[pl.ds(pl.multiple_of(place * share, share), share)] = ref[...]


def first_body(flags, slot_block, high, low, *refs):
    blocks, (rhs, keep, send, x, current, sem) = refs[:8], refs[8:]
    copy = pltpu.make_async_copy(rhs.at[0], current, sem)
    copy.start()
    rank = lax.axis_index("row")
    core = bit(rank, 0)
    assemble(x, blocks, rank)
    parts = split(x[...])
    weight = flags[0, 0].astype(jnp.float32)
    size = keep.shape[0]
    copy.wait()
    for out, part in ((send, 1 - core), (keep, core)):
        rows = pl.ds(pl.multiple_of(part * size, size), size)
        new = current[rows] - weight * dot3((high[rows], low[rows]), parts)
        out[...] = jnp.where(slot_block[rank] == 0, x[rows], new)


def second_body(flags, slot_block, high, low, *refs):
    blocks, (keep, send, out, x) = refs[:8], refs[8:]
    rank = lax.axis_index("row")
    core, held = bit(rank, 0), slot_block[rank]
    assemble(x, blocks, rank)
    parts = split(x[...])
    weight = flags[0, 1].astype(jnp.float32)
    size = keep.shape[0]
    for current, part in ((keep, core), (send, 1 - core)):
        rows = pl.ds(pl.multiple_of(part * size, size), size)
        new = current[...] - weight * dot3((high[rows], low[rows]), parts)
        out[rows] = jnp.where(held == 0, current[...], jnp.where(held == 1, x[rows], new))


def solve_body(inverse, *refs):
    quarters, (out, y) = refs[:4], refs[4:]
    rank = lax.axis_index("row")
    size = quarters[0].shape[0]
    core, z = bit(rank, 0), bit(rank, 1)
    for index, ref in enumerate(quarters):
        place = (core ^ (index >> 1)) * 2 + (z ^ (index & 1))
        y[pl.ds(pl.multiple_of(place * size, size), size)] = ref[...]
    out[...] = dot3(split(inverse[...]), split(y[...]))


def solve(inverse, quarters):
    rows, depth = inverse.shape
    cols = quarters[0].shape[1]
    vmem = pl.BlockSpec(memory_space=pltpu.VMEM)
    return pl.pallas_call(
        solve_body,
        out_shape=jax.ShapeDtypeStruct((rows, cols), jnp.float32),
        in_specs=[vmem] * 5,
        out_specs=vmem,
        scratch_shapes=[pltpu.VMEM((depth, cols), jnp.float32)],
        compiler_params=pltpu.CompilerParams(vmem_limit_bytes=UPDATE_BYTES),
        cost_estimate=pl.CostEstimate(flops=2 * rows * depth * cols, bytes_accessed=4 * rows * cols, transcendentals=0),
        name="solve",
    )(inverse, *quarters)


def update(step, flags, slot_block, pair, blocks, current):
    depth = pair[0].shape[1]
    rows, cols = pair[0].shape[0], blocks[0].shape[1]
    vmem, smem = pl.BlockSpec(memory_space=pltpu.VMEM), pl.BlockSpec(memory_space=pltpu.SMEM)
    counts = (rows // 2, rows // 2) if step == 0 else (rows,)
    scratch = [pltpu.VMEM((depth, cols), jnp.float32)]
    if step == 0:
        scratch += [pltpu.VMEM((rows, cols), jnp.float32), pltpu.SemaphoreType.DMA]
    return pl.pallas_call(
        first_body if step == 0 else second_body,
        out_shape=[jax.ShapeDtypeStruct((count, cols), jnp.float32) for count in counts],
        in_specs=[smem, smem] + [vmem] * 10 + ([pl.BlockSpec(memory_space=pl.ANY)] if step == 0 else [vmem] * 2),
        out_specs=[vmem] * len(counts),
        scratch_shapes=scratch,
        compiler_params=pltpu.CompilerParams(vmem_limit_bytes=UPDATE_BYTES),
        cost_estimate=pl.CostEstimate(flops=6 * rows * depth * cols, bytes_accessed=4 * rows * (depth + 3 * cols), transcendentals=0),
        name="update",
    )(flags, slot_block, *pair, *blocks, *current)


def general(rows, cols, rhs, panel, diag_inverse, flags, slot_block):
    rank = lax.axis_index("row")
    owners = (jnp.argmax(slot_block == 0), jnp.argmax(slot_block == 1))
    weights = flags[0].astype(jnp.float32)
    bits = rows.bit_length() - 1
    current = rhs[0]
    solved = []
    for step in range(2):
        pivot = current
        for b in range(bits - 1):
            pivot = scatter_step(pivot, b, rows, owners[step], rank)
        pivot = cross_step(pivot, bits - 1, rows, owners[step], rank)
        for b in reversed(range(bits - 1)):
            pivot = gather_step(pivot, b, rows, rank)
        x = jnp.dot(diag_inverse[step], pivot, precision=HIGH)
        for b in range(bits):
            x = gather_step(x, b, rows, rank)
        whole = lax.all_gather(panel[0, step], "col", axis=0, tiled=True)
        current = current - weights[step] * jnp.dot(whole, x, precision=HIGH)
        solved.append(x)
    held = slot_block[rank]
    return jnp.where(held == 0, solved[0], jnp.where(held == 1, solved[1], current))[None]


def paced(rows, cols, rhs, panel, diag_inverse, flags, slot_block):
    rank = lax.axis_index("row")
    owner, second = jnp.argmax(slot_block == 0), jnp.argmax(slot_block == 1)
    half = panel.shape[2] // 2
    core = bit(rank, 0)

    def near(one, two):
        return [swap(one, "col", 0, cols), swap(two, "col", 1, cols)]

    def far(one, two):
        return [swap(one, "col", 1, cols), swap(two, "col", 0, cols)]

    def block_halves(panel, step):
        return panel[0, step, :half], panel[0, step, half:]

    def solved(step, y, panel, owner):
        y, panel = tie(y, panel)
        block = tie(*block_halves(panel, step))
        first = near(*block)
        y = scatter_step(y, 1, rows, owner, rank)
        y, *block = tie(y, *block)
        second = near(*block[::-1])
        y = cross_step(y, 2, rows, owner, rank)
        y, inverse, *first = tie(y, diag_inverse, *first)
        pieces = far(*first)
        beside = swap(y, "row", 1, rows)
        y, *second = tie(y, *second)
        other = swap(y, "row", 0, rows)
        beside, inverse = tie(beside, inverse[step])
        last = swap(beside, "row", 0, rows)
        x = solve(inverse, [y, beside, other, last])
        x2, x1 = swap(x, "row", 2, rows), swap(x, "row", 1, rows)
        x2, x1, *pieces = tie(x2, x1, *pieces)
        high, low = prepare([*block, *first, *second, *pieces])
        x3 = swap(x2, "row", 1, rows)
        across = [swap(block, "row", 0, rows) for block in (x, x1, x2)]
        x3, high, low, *across = tie(x3, high, low, *across)
        return [x, x1, x2, x3, *across, swap(x3, "row", 0, rows)], (high, low)

    send, keep = cut(rhs)
    got = swap(send, "row", 0, rows)
    y = jnp.where(bit(owner, 0) == core, keep, got)
    blocks, pair = solved(0, y, panel, owner)
    keep, send = update(0, flags, slot_block, pair, blocks, [rhs])
    got = swap(send, "row", 0, rows)
    y = jnp.where(bit(second, 0) == core, keep, got)
    blocks, pair = solved(1, y, panel, second)
    (result,) = update(1, flags, slot_block, pair, blocks, [keep, send])
    return result[None]


def solution(mesh):
    rows, cols = mesh.shape["row"], mesh.shape["col"]
    form = paced if (rows, cols) == (8, 4) else general

    def shards(*args):
        return form(rows, cols, *args)

    in_specs = (
        P("row", None, "col"),
        P("row", None, "col", None),
        P(None, "row", None),
        P("row", None),
        P(),
    )
    out_specs = P("row", None, "col")
    return jax.shard_map(shards, mesh=mesh, in_specs=in_specs, out_specs=out_specs, check_vma=False)
```

```python
import functools

import jax
import jax.numpy as jnp
from jax import lax
from jax.experimental import pallas as pl
from jax.experimental.pallas import tpu as pltpu
from jax.sharding import PartitionSpec as P

HIGH = lax.Precision.HIGH
PREPARE_BYTES = 4 * 2**20
UPDATE_BYTES = 5 * 2**20


def bit(index, b):
    return (index >> b) & 1


def swap(x, axis, b, size):
    return lax.ppermute(x, axis, [(i, i ^ (1 << b)) for i in range(size)])


def tie(value, *others):
    return lax.optimization_barrier((value, *others))


def join(low_first, a, b):
    return jnp.where(low_first, jnp.concatenate([a, b]), jnp.concatenate([b, a]))


def halves(x, b):
    half = x.shape[0] // 2
    return lax.dynamic_slice_in_dim(x, b * half, half), lax.dynamic_slice_in_dim(x, (1 - b) * half, half)


def scatter_step(x, b, size, owner, me):
    mine = bit(me, b)
    keep, send = halves(x, mine)
    return jnp.where(bit(owner, b) == mine, keep, swap(send, "row", b, size))


def cross_step(x, b, size, owner, me):
    return jnp.where(bit(owner, b) == bit(me, b), x, swap(x, "row", b, size))


def gather_step(x, b, size, me):
    return join(bit(me, b) == 0, x, swap(x, "row", b, size))


def split(x):
    high = x.astype(jnp.bfloat16)
    return high, (x - high.astype(jnp.float32)).astype(jnp.bfloat16)


def dot3(a, b):
    def dot(p, q):
        return jnp.dot(p, q, preferred_element_type=jnp.float32)

    return dot(a[0], b[0]) + (dot(a[0], b[1]) + dot(a[1], b[0]))


def prepare_body(own_top, own_bottom, *refs):
    pieces, (high, low, slots, sems) = refs[:6], refs[6:]
    side = lax.axis_index("col")
    half = pieces[0].shape[0]
    sources = [(own_top, side * 2), (own_bottom, side * 2 + 1)]
    for ref, (distance, part) in zip(pieces, ((1, 0), (2, 1), (1, 1), (2, 0), (3, 0), (3, 1))):
        sources.append((ref, (side ^ distance) * 2 + part))
    groups = [sources[start:start + 2] for start in range(0, 8, 2)]

    def fetch(index):
        copies = []
        start = 0
        for member, (ref, _) in enumerate(groups[index]):
            into = slots.at[index % 2, pl.ds(start, ref.shape[0])]
            copies.append(pltpu.make_async_copy(ref, into, sems.at[index % 2, member]))
            start += ref.shape[0]
        for copy in copies:
            copy.start()
        return copies

    flying = [fetch(0), fetch(1)]
    for index, group in enumerate(groups):
        for copy in flying[index]:
            copy.wait()
        start = 0
        for ref, place in group:
            rows = pl.ds(pl.multiple_of(place * half, half), ref.shape[0])
            high[rows], low[rows] = split(slots[index % 2, pl.ds(start, ref.shape[0])])
            start += ref.shape[0]
        if index + 2 < len(groups):
            flying.append(fetch(index + 2))


def prepare(pieces):
    half, depth = pieces[0].shape
    vmem, anywhere = pl.BlockSpec(memory_space=pltpu.VMEM), pl.BlockSpec(memory_space=pl.ANY)
    return pl.pallas_call(
        prepare_body,
        out_shape=[jax.ShapeDtypeStruct((depth, depth), jnp.bfloat16)] * 2,
        in_specs=[anywhere] * 8,
        out_specs=[vmem] * 2,
        scratch_shapes=[pltpu.VMEM((2, 2 * half, depth), jnp.float32), pltpu.SemaphoreType.DMA((2, 2))],
        compiler_params=pltpu.CompilerParams(vmem_limit_bytes=PREPARE_BYTES),
        cost_estimate=pl.CostEstimate(flops=0, bytes_accessed=16 * depth * depth, transcendentals=0),
        name="prepare",
    )(*pieces)


def assemble(x, blocks, rank):
    core, z = bit(rank, 0), rank >> 1
    share = blocks[0].shape[0]
    for index, ref in enumerate(blocks):
        place = (z ^ (index & 3)) * 2 + (core ^ (index >> 2))
        x[pl.ds(pl.multiple_of(place * share, share), share)] = ref[...]


def first_body(flags, slot_block, high, low, *refs):
    blocks, (rhs, keep, send, x, current, sem) = refs[:8], refs[8:]
    copy = pltpu.make_async_copy(rhs.at[0], current, sem)
    copy.start()
    rank = lax.axis_index("row")
    core = bit(rank, 0)
    assemble(x, blocks, rank)
    parts = split(x[...])
    weight = flags[0, 0].astype(jnp.float32)
    size = keep.shape[0]
    copy.wait()
    for out, part in ((send, 1 - core), (keep, core)):
        rows = pl.ds(pl.multiple_of(part * size, size), size)
        new = current[rows] - weight * dot3((high[rows], low[rows]), parts)
        out[...] = jnp.where(slot_block[rank] == 0, x[rows], new)


def second_body(flags, slot_block, high, low, *refs):
    blocks, (keep, send, out, x) = refs[:8], refs[8:]
    rank = lax.axis_index("row")
    core, held = bit(rank, 0), slot_block[rank]
    assemble(x, blocks, rank)
    parts = split(x[...])
    weight = flags[0, 1].astype(jnp.float32)
    size = keep.shape[0]
    for current, part in ((keep, core), (send, 1 - core)):
        rows = pl.ds(pl.multiple_of(part * size, size), size)
        new = current[...] - weight * dot3((high[rows], low[rows]), parts)
        out[rows] = jnp.where(held == 0, current[...], jnp.where(held == 1, x[rows], new))


def solve_body(inverse, *refs):
    quarters, (out, y) = refs[:4], refs[4:]
    rank = lax.axis_index("row")
    size = quarters[0].shape[0]
    core, z = bit(rank, 0), bit(rank, 1)
    for index, ref in enumerate(quarters):
        place = (core ^ (index >> 1)) * 2 + (z ^ (index & 1))
        y[pl.ds(pl.multiple_of(place * size, size), size)] = ref[...]
    out[...] = dot3(split(inverse[...]), split(y[...]))


def solve(inverse, quarters):
    rows, depth = inverse.shape
    cols = quarters[0].shape[1]
    vmem = pl.BlockSpec(memory_space=pltpu.VMEM)
    return pl.pallas_call(
        solve_body,
        out_shape=jax.ShapeDtypeStruct((rows, cols), jnp.float32),
        in_specs=[vmem] * 5,
        out_specs=vmem,
        scratch_shapes=[pltpu.VMEM((depth, cols), jnp.float32)],
        compiler_params=pltpu.CompilerParams(vmem_limit_bytes=UPDATE_BYTES),
        cost_estimate=pl.CostEstimate(flops=2 * rows * depth * cols, bytes_accessed=4 * rows * cols, transcendentals=0),
        name="solve",
    )(inverse, *quarters)


def update(step, flags, slot_block, pair, blocks, current):
    depth = pair[0].shape[1]
    rows, cols = pair[0].shape[0], blocks[0].shape[1]
    vmem, smem = pl.BlockSpec(memory_space=pltpu.VMEM), pl.BlockSpec(memory_space=pltpu.SMEM)
    counts = (rows // 2, rows // 2) if step == 0 else (rows,)
    scratch = [pltpu.VMEM((depth, cols), jnp.float32)]
    if step == 0:
        scratch += [pltpu.VMEM((rows, cols), jnp.float32), pltpu.SemaphoreType.DMA]
    return pl.pallas_call(
        first_body if step == 0 else second_body,
        out_shape=[jax.ShapeDtypeStruct((count, cols), jnp.float32) for count in counts],
        in_specs=[smem, smem] + [vmem] * 10 + ([pl.BlockSpec(memory_space=pl.ANY)] if step == 0 else [vmem] * 2),
        out_specs=[vmem] * len(counts),
        scratch_shapes=scratch,
        compiler_params=pltpu.CompilerParams(vmem_limit_bytes=UPDATE_BYTES),
        cost_estimate=pl.CostEstimate(flops=6 * rows * depth * cols, bytes_accessed=4 * rows * (depth + 3 * cols), transcendentals=0),
        name="update",
    )(flags, slot_block, *pair, *blocks, *current)


def general(rows, cols, rhs, panel, diag_inverse, flags, slot_block):
    rank = lax.axis_index("row")
    owners = (jnp.argmax(slot_block == 0), jnp.argmax(slot_block == 1))
    weights = flags[0].astype(jnp.float32)
    bits = rows.bit_length() - 1
    current = rhs[0]
    solved = []
    for step in range(2):
        pivot = current
        for b in range(bits - 1):
            pivot = scatter_step(pivot, b, rows, owners[step], rank)
        pivot = cross_step(pivot, bits - 1, rows, owners[step], rank)
        for b in reversed(range(bits - 1)):
            pivot = gather_step(pivot, b, rows, rank)
        x = jnp.dot(diag_inverse[step], pivot, precision=HIGH)
        for b in range(bits):
            x = gather_step(x, b, rows, rank)
        whole = lax.all_gather(panel[0, step], "col", axis=0, tiled=True)
        current = current - weights[step] * jnp.dot(whole, x, precision=HIGH)
        solved.append(x)
    held = slot_block[rank]
    return jnp.where(held == 0, solved[0], jnp.where(held == 1, solved[1], current))[None]


def paced(rows, cols, rhs, panel, diag_inverse, flags, slot_block):
    rank = lax.axis_index("row")
    owner, second = jnp.argmax(slot_block == 0), jnp.argmax(slot_block == 1)
    half = panel.shape[2] // 2
    core = bit(rank, 0)

    def near(one, two):
        return [swap(one, "col", 0, cols), swap(two, "col", 1, cols)]

    def far(one, two):
        return [swap(one, "col", 1, cols), swap(two, "col", 0, cols)]

    def block_halves(panel, step):
        return panel[0, step, :half], panel[0, step, half:]

    def solved(step, y, panel, owner):
        y, panel = tie(y, panel)
        block = tie(*block_halves(panel, step))
        first = near(*block)
        y = scatter_step(y, 1, rows, owner, rank)
        y, *block = tie(y, *block)
        second = near(*block[::-1])
        y = cross_step(y, 2, rows, owner, rank)
        y, inverse, *first = tie(y, diag_inverse, *first)
        pieces = far(*first)
        beside = swap(y, "row", 1, rows)
        y, *second = tie(y, *second)
        other = swap(y, "row", 0, rows)
        beside, inverse = tie(beside, inverse[step])
        last = swap(beside, "row", 0, rows)
        x = solve(inverse, [y, beside, other, last])
        x2, x1 = swap(x, "row", 2, rows), swap(x, "row", 1, rows)
        x2, x1, *pieces = tie(x2, x1, *pieces)
        high, low = prepare([*block, *first, *second, *pieces])
        x3 = swap(x2, "row", 1, rows)
        across = [swap(block, "row", 0, rows) for block in (x, x1, x2)]
        x3, high, low, *across = tie(x3, high, low, *across)
        return [x, x1, x2, x3, *across, swap(x3, "row", 0, rows)], (high, low)

    keep, send = halves(rhs[0], core)
    got = swap(send, "row", 0, rows)
    keep, send = tie(keep, send)
    y = jnp.where(bit(owner, 0) == core, keep, got)
    blocks, pair = solved(0, y, panel, owner)
    keep, send = update(0, flags, slot_block, pair, blocks, [rhs])
    got = swap(send, "row", 0, rows)
    y = jnp.where(bit(second, 0) == core, keep, got)
    blocks, pair = solved(1, y, panel, second)
    (result,) = update(1, flags, slot_block, pair, blocks, [keep, send])
    return result[None]


def solution(mesh):
    rows, cols = mesh.shape["row"], mesh.shape["col"]
    form = paced if (rows, cols) == (8, 4) else general

    def shards(*args):
        return form(rows, cols, *args)

    in_specs = (
        P("row", None, "col"),
        P("row", None, "col", None),
        P(None, "row", None),
        P("row", None),
        P(),
    )
    out_specs = P("row", None, "col")
    return jax.shard_map(shards, mesh=mesh, in_specs=in_specs, out_specs=out_specs, check_vma=False)
```

```python
import functools

import jax
import jax.numpy as jnp
from jax import lax
from jax.experimental import pallas as pl
from jax.experimental.pallas import tpu as pltpu
from jax.sharding import PartitionSpec as P

HIGH = lax.Precision.HIGH
PREPARE_BYTES = 4 * 2**20
UPDATE_BYTES = 5 * 2**20


def bit(index, b):
    return (index >> b) & 1


def swap(x, axis, b, size):
    return lax.ppermute(x, axis, [(i, i ^ (1 << b)) for i in range(size)])


def tie(value, *others):
    return lax.optimization_barrier((value, *others))


def join(low_first, a, b):
    return jnp.where(low_first, jnp.concatenate([a, b]), jnp.concatenate([b, a]))


def halves(x, b):
    half = x.shape[0] // 2
    return lax.dynamic_slice_in_dim(x, b * half, half), lax.dynamic_slice_in_dim(x, (1 - b) * half, half)


def scatter_step(x, b, size, owner, me):
    mine = bit(me, b)
    keep, send = halves(x, mine)
    return jnp.where(bit(owner, b) == mine, keep, swap(send, "row", b, size))


def cross_step(x, b, size, owner, me):
    return jnp.where(bit(owner, b) == bit(me, b), x, swap(x, "row", b, size))


def gather_step(x, b, size, me):
    return join(bit(me, b) == 0, x, swap(x, "row", b, size))


def split(x):
    high = x.astype(jnp.bfloat16)
    return high, (x - high.astype(jnp.float32)).astype(jnp.bfloat16)


def dot3(a, b):
    def dot(p, q):
        return jnp.dot(p, q, preferred_element_type=jnp.float32)

    return dot(a[0], b[0]) + (dot(a[0], b[1]) + dot(a[1], b[0]))


def prepare_body(own_top, own_bottom, *refs):
    pieces, (high, low, slots, sems) = refs[:6], refs[6:]
    side = lax.axis_index("col")
    half = pieces[0].shape[0]
    sources = [(own_top, side * 2), (own_bottom, side * 2 + 1)]
    for ref, (distance, part) in zip(pieces, ((1, 0), (2, 1), (1, 1), (2, 0), (3, 0), (3, 1))):
        sources.append((ref, (side ^ distance) * 2 + part))
    groups = [sources[start:start + 2] for start in range(0, 8, 2)]

    def fetch(index):
        copies = []
        start = 0
        for member, (ref, _) in enumerate(groups[index]):
            into = slots.at[index % 2, pl.ds(start, ref.shape[0])]
            copies.append(pltpu.make_async_copy(ref, into, sems.at[index % 2, member]))
            start += ref.shape[0]
        for copy in copies:
            copy.start()
        return copies

    flying = [fetch(0), fetch(1)]
    for index, group in enumerate(groups):
        for copy in flying[index]:
            copy.wait()
        start = 0
        for ref, place in group:
            rows = pl.ds(pl.multiple_of(place * half, half), ref.shape[0])
            high[rows], low[rows] = split(slots[index % 2, pl.ds(start, ref.shape[0])])
            start += ref.shape[0]
        if index + 2 < len(groups):
            flying.append(fetch(index + 2))


def prepare(pieces):
    half, depth = pieces[0].shape
    vmem, anywhere = pl.BlockSpec(memory_space=pltpu.VMEM), pl.BlockSpec(memory_space=pl.ANY)
    return pl.pallas_call(
        prepare_body,
        out_shape=[jax.ShapeDtypeStruct((depth, depth), jnp.bfloat16)] * 2,
        in_specs=[anywhere] * 8,
        out_specs=[vmem] * 2,
        scratch_shapes=[pltpu.VMEM((2, 2 * half, depth), jnp.float32), pltpu.SemaphoreType.DMA((2, 2))],
        compiler_params=pltpu.CompilerParams(vmem_limit_bytes=PREPARE_BYTES),
        cost_estimate=pl.CostEstimate(flops=0, bytes_accessed=16 * depth * depth, transcendentals=0),
        name="prepare",
    )(*pieces)


def assemble(x, blocks, rank):
    core, z = bit(rank, 0), rank >> 1
    share = blocks[0].shape[0]
    for index, ref in enumerate(blocks):
        place = (z ^ (index & 3)) * 2 + (core ^ (index >> 2))
        x[pl.ds(pl.multiple_of(place * share, share), share)] = ref[...]


def first_body(flags, slot_block, high, low, *refs):
    blocks, (rhs, keep, send, x, current, sem) = refs[:8], refs[8:]
    copy = pltpu.make_async_copy(rhs.at[0], current, sem)
    copy.start()
    rank = lax.axis_index("row")
    core = bit(rank, 0)
    assemble(x, blocks, rank)
    parts = split(x[...])
    weight = flags[0, 0].astype(jnp.float32)
    size = keep.shape[0]
    copy.wait()
    for out, part in ((send, 1 - core), (keep, core)):
        rows = pl.ds(pl.multiple_of(part * size, size), size)
        new = current[rows] - weight * dot3((high[rows], low[rows]), parts)
        out[...] = jnp.where(slot_block[rank] == 0, x[rows], new)


def second_body(flags, slot_block, high, low, *refs):
    blocks, (keep, send, out, x) = refs[:8], refs[8:]
    rank = lax.axis_index("row")
    core, held = bit(rank, 0), slot_block[rank]
    assemble(x, blocks, rank)
    parts = split(x[...])
    weight = flags[0, 1].astype(jnp.float32)
    size = keep.shape[0]
    for current, part in ((keep, core), (send, 1 - core)):
        rows = pl.ds(pl.multiple_of(part * size, size), size)
        new = current[...] - weight * dot3((high[rows], low[rows]), parts)
        out[rows] = jnp.where(held == 0, current[...], jnp.where(held == 1, x[rows], new))


def solve_body(inverse, *refs):
    quarters, (out, y) = refs[:4], refs[4:]
    rank = lax.axis_index("row")
    size = quarters[0].shape[0]
    core, z = bit(rank, 0), bit(rank, 1)
    for index, ref in enumerate(quarters):
        place = (core ^ (index >> 1)) * 2 + (z ^ (index & 1))
        y[pl.ds(pl.multiple_of(place * size, size), size)] = ref[...]
    out[...] = dot3(split(inverse[...]), split(y[...]))


def solve(inverse, quarters):
    rows, depth = inverse.shape
    cols = quarters[0].shape[1]
    vmem = pl.BlockSpec(memory_space=pltpu.VMEM)
    return pl.pallas_call(
        solve_body,
        out_shape=jax.ShapeDtypeStruct((rows, cols), jnp.float32),
        in_specs=[vmem] * 5,
        out_specs=vmem,
        scratch_shapes=[pltpu.VMEM((depth, cols), jnp.float32)],
        compiler_params=pltpu.CompilerParams(vmem_limit_bytes=UPDATE_BYTES),
        cost_estimate=pl.CostEstimate(flops=2 * rows * depth * cols, bytes_accessed=4 * rows * cols, transcendentals=0),
        name="solve",
    )(inverse, *quarters)


def update(step, flags, slot_block, pair, blocks, current):
    depth = pair[0].shape[1]
    rows, cols = pair[0].shape[0], blocks[0].shape[1]
    vmem, smem = pl.BlockSpec(memory_space=pltpu.VMEM), pl.BlockSpec(memory_space=pltpu.SMEM)
    counts = (rows // 2, rows // 2) if step == 0 else (rows,)
    scratch = [pltpu.VMEM((depth, cols), jnp.float32)]
    if step == 0:
        scratch += [pltpu.VMEM((rows, cols), jnp.float32), pltpu.SemaphoreType.DMA]
    return pl.pallas_call(
        first_body if step == 0 else second_body,
        out_shape=[jax.ShapeDtypeStruct((count, cols), jnp.float32) for count in counts],
        in_specs=[smem, smem] + [vmem] * 10 + ([pl.BlockSpec(memory_space=pl.ANY)] if step == 0 else [vmem] * 2),
        out_specs=[vmem] * len(counts),
        scratch_shapes=scratch,
        compiler_params=pltpu.CompilerParams(vmem_limit_bytes=UPDATE_BYTES),
        cost_estimate=pl.CostEstimate(flops=6 * rows * depth * cols, bytes_accessed=4 * rows * (depth + 3 * cols), transcendentals=0),
        name="update",
    )(flags, slot_block, *pair, *blocks, *current)


def general(rows, cols, rhs, panel, diag_inverse, flags, slot_block):
    rank = lax.axis_index("row")
    owners = (jnp.argmax(slot_block == 0), jnp.argmax(slot_block == 1))
    weights = flags[0].astype(jnp.float32)
    bits = rows.bit_length() - 1
    current = rhs[0]
    solved = []
    for step in range(2):
        pivot = current
        for b in range(bits - 1):
            pivot = scatter_step(pivot, b, rows, owners[step], rank)
        pivot = cross_step(pivot, bits - 1, rows, owners[step], rank)
        for b in reversed(range(bits - 1)):
            pivot = gather_step(pivot, b, rows, rank)
        x = jnp.dot(diag_inverse[step], pivot, precision=HIGH)
        for b in range(bits):
            x = gather_step(x, b, rows, rank)
        whole = lax.all_gather(panel[0, step], "col", axis=0, tiled=True)
        current = current - weights[step] * jnp.dot(whole, x, precision=HIGH)
        solved.append(x)
    held = slot_block[rank]
    return jnp.where(held == 0, solved[0], jnp.where(held == 1, solved[1], current))[None]


def paced(rows, cols, rhs, panel, diag_inverse, flags, slot_block):
    rank = lax.axis_index("row")
    owner, second = jnp.argmax(slot_block == 0), jnp.argmax(slot_block == 1)
    half = panel.shape[2] // 2
    core = bit(rank, 0)

    def near(one, two):
        return [swap(one, "col", 0, cols), swap(two, "col", 1, cols)]

    def far(one, two):
        return [swap(one, "col", 1, cols), swap(two, "col", 0, cols)]

    def block_halves(panel, step):
        return panel[0, step, :half], panel[0, step, half:]

    def solved(step, y, panel, owner):
        y, panel = tie(y, panel)
        block = tie(*block_halves(panel, step))
        first = near(*block)
        y = scatter_step(y, 1, rows, owner, rank)
        y, *block = tie(y, *block)
        second = near(*block[::-1])
        y = cross_step(y, 2, rows, owner, rank)
        y, inverse, *first = tie(y, diag_inverse, *first)
        pieces = far(*first)
        beside = swap(y, "row", 1, rows)
        y, *second = tie(y, *second)
        other = swap(y, "row", 0, rows)
        beside, inverse = tie(beside, inverse[step])
        last = swap(beside, "row", 0, rows)
        x = solve(inverse, [y, beside, other, last])
        x2, x1 = swap(x, "row", 2, rows), swap(x, "row", 1, rows)
        x2, x1, *pieces = tie(x2, x1, *pieces)
        high, low = prepare([*block, *first, *second, *pieces])
        x3 = swap(x2, "row", 1, rows)
        across = [swap(block, "row", 0, rows) for block in (x, x1, x2)]
        x3, high, low, *across = tie(x3, high, low, *across)
        return [x, x1, x2, x3, *across, swap(x3, "row", 0, rows)], (high, low)

    got = swap(rhs, "row", 0, rows)
    y = jnp.where(bit(owner, 0) == core, halves(rhs[0], core)[0], halves(got[0], core)[0])
    blocks, pair = solved(0, y, panel, owner)
    keep, send = update(0, flags, slot_block, pair, blocks, [rhs])
    got = swap(send, "row", 0, rows)
    y = jnp.where(bit(second, 0) == core, keep, got)
    blocks, pair = solved(1, y, panel, second)
    (result,) = update(1, flags, slot_block, pair, blocks, [keep, send])
    return result[None]


def solution(mesh):
    rows, cols = mesh.shape["row"], mesh.shape["col"]
    form = paced if (rows, cols) == (8, 4) else general

    def shards(*args):
        return form(rows, cols, *args)

    in_specs = (
        P("row", None, "col"),
        P("row", None, "col", None),
        P(None, "row", None),
        P("row", None),
        P(),
    )
    out_specs = P("row", None, "col")
    return jax.shard_map(shards, mesh=mesh, in_specs=in_specs, out_specs=out_specs, check_vma=False)
```

```python
import functools

import jax
import jax.numpy as jnp
from jax import lax
from jax.experimental import pallas as pl
from jax.experimental.pallas import tpu as pltpu
from jax.sharding import PartitionSpec as P

HIGH = lax.Precision.HIGH
PREPARE_BYTES = 4 * 2**20
UPDATE_BYTES = 5 * 2**20


def bit(index, b):
    return (index >> b) & 1


def swap(x, axis, b, size):
    return lax.ppermute(x, axis, [(i, i ^ (1 << b)) for i in range(size)])


def tie(value, *others):
    return lax.optimization_barrier((value, *others))


def join(low_first, a, b):
    return jnp.where(low_first, jnp.concatenate([a, b]), jnp.concatenate([b, a]))


def halves(x, b):
    half = x.shape[0] // 2
    return lax.dynamic_slice_in_dim(x, b * half, half), lax.dynamic_slice_in_dim(x, (1 - b) * half, half)


def scatter_step(x, b, size, owner, me):
    mine = bit(me, b)
    keep, send = halves(x, mine)
    return jnp.where(bit(owner, b) == mine, keep, swap(send, "row", b, size))


def cross_step(x, b, size, owner, me):
    return jnp.where(bit(owner, b) == bit(me, b), x, swap(x, "row", b, size))


def gather_step(x, b, size, me):
    return join(bit(me, b) == 0, x, swap(x, "row", b, size))


def split(x):
    high = x.astype(jnp.bfloat16)
    return high, (x - high.astype(jnp.float32)).astype(jnp.bfloat16)


def dot3(a, b):
    def dot(p, q):
        return jnp.dot(p, q, preferred_element_type=jnp.float32)

    return dot(a[0], b[0]) + (dot(a[0], b[1]) + dot(a[1], b[0]))


def prepare_body(own_top, own_bottom, *refs):
    pieces, (high, low, slots, sems) = refs[:6], refs[6:]
    side = lax.axis_index("col")
    half = pieces[0].shape[0]
    sources = [(own_top, side * 2), (own_bottom, side * 2 + 1)]
    for ref, (distance, part) in zip(pieces, ((1, 0), (2, 1), (1, 1), (2, 0), (3, 0), (3, 1))):
        sources.append((ref, (side ^ distance) * 2 + part))
    groups = [sources[start:start + 2] for start in range(0, 8, 2)]

    def fetch(index):
        copies = []
        start = 0
        for member, (ref, _) in enumerate(groups[index]):
            into = slots.at[index % 2, pl.ds(start, ref.shape[0])]
            copies.append(pltpu.make_async_copy(ref, into, sems.at[index % 2, member]))
            start += ref.shape[0]
        for copy in copies:
            copy.start()
        return copies

    flying = [fetch(0), fetch(1)]
    for index, group in enumerate(groups):
        for copy in flying[index]:
            copy.wait()
        start = 0
        for ref, place in group:
            rows = pl.ds(pl.multiple_of(place * half, half), ref.shape[0])
            high[rows], low[rows] = split(slots[index % 2, pl.ds(start, ref.shape[0])])
            start += ref.shape[0]
        if index + 2 < len(groups):
            flying.append(fetch(index + 2))


def prepare(pieces):
    half, depth = pieces[0].shape
    vmem, anywhere = pl.BlockSpec(memory_space=pltpu.VMEM), pl.BlockSpec(memory_space=pl.ANY)
    return pl.pallas_call(
        prepare_body,
        out_shape=[jax.ShapeDtypeStruct((depth, depth), jnp.bfloat16)] * 2,
        in_specs=[anywhere] * 8,
        out_specs=[vmem] * 2,
        scratch_shapes=[pltpu.VMEM((2, 2 * half, depth), jnp.float32), pltpu.SemaphoreType.DMA((2, 2))],
        compiler_params=pltpu.CompilerParams(vmem_limit_bytes=PREPARE_BYTES),
        cost_estimate=pl.CostEstimate(flops=0, bytes_accessed=16 * depth * depth, transcendentals=0),
        name="prepare",
    )(*pieces)


def assemble(x, blocks, rank):
    core, z = bit(rank, 0), rank >> 1
    share = blocks[0].shape[0]
    for index, ref in enumerate(blocks):
        place = (z ^ (index & 3)) * 2 + (core ^ (index >> 2))
        x[pl.ds(pl.multiple_of(place * share, share), share)] = ref[...]


def first_body(flags, slot_block, high, low, *refs):
    blocks, (rhs, keep, send, x, current, sem) = refs[:8], refs[8:]
    copy = pltpu.make_async_copy(rhs.at[0], current, sem)
    copy.start()
    rank = lax.axis_index("row")
    core = bit(rank, 0)
    assemble(x, blocks, rank)
    parts = split(x[...])
    weight = flags[0, 0].astype(jnp.float32)
    size = keep.shape[0]
    copy.wait()
    for out, part in ((send, 1 - core), (keep, core)):
        rows = pl.ds(pl.multiple_of(part * size, size), size)
        new = current[rows] - weight * dot3((high[rows], low[rows]), parts)
        out[...] = jnp.where(slot_block[rank] == 0, x[rows], new)


def second_body(flags, slot_block, high, low, *refs):
    blocks, (keep, send, out, x) = refs[:8], refs[8:]
    rank = lax.axis_index("row")
    core, held = bit(rank, 0), slot_block[rank]
    assemble(x, blocks, rank)
    parts = split(x[...])
    weight = flags[0, 1].astype(jnp.float32)
    size = keep.shape[0]
    for current, part in ((keep, core), (send, 1 - core)):
        rows = pl.ds(pl.multiple_of(part * size, size), size)
        new = current[...] - weight * dot3((high[rows], low[rows]), parts)
        out[rows] = jnp.where(held == 0, current[...], jnp.where(held == 1, x[rows], new))


def solve_body(inverse, *refs):
    quarters, (out, y) = refs[:4], refs[4:]
    rank = lax.axis_index("row")
    size = quarters[0].shape[0]
    core, z = bit(rank, 0), bit(rank, 1)
    for index, ref in enumerate(quarters):
        place = (core ^ (index >> 1)) * 2 + (z ^ (index & 1))
        y[pl.ds(pl.multiple_of(place * size, size), size)] = ref[...]
    out[...] = dot3(split(inverse[...]), split(y[...]))


def solve(inverse, quarters):
    rows, depth = inverse.shape
    cols = quarters[0].shape[1]
    vmem = pl.BlockSpec(memory_space=pltpu.VMEM)
    return pl.pallas_call(
        solve_body,
        out_shape=jax.ShapeDtypeStruct((rows, cols), jnp.float32),
        in_specs=[vmem] * 5,
        out_specs=vmem,
        scratch_shapes=[pltpu.VMEM((depth, cols), jnp.float32)],
        compiler_params=pltpu.CompilerParams(vmem_limit_bytes=UPDATE_BYTES),
        cost_estimate=pl.CostEstimate(flops=2 * rows * depth * cols, bytes_accessed=4 * rows * cols, transcendentals=0),
        name="solve",
    )(inverse, *quarters)


def update(step, flags, slot_block, pair, blocks, current):
    depth = pair[0].shape[1]
    rows, cols = pair[0].shape[0], blocks[0].shape[1]
    vmem, smem = pl.BlockSpec(memory_space=pltpu.VMEM), pl.BlockSpec(memory_space=pltpu.SMEM)
    counts = (rows // 2, rows // 2) if step == 0 else (rows,)
    scratch = [pltpu.VMEM((depth, cols), jnp.float32)]
    if step == 0:
        scratch += [pltpu.VMEM((rows, cols), jnp.float32), pltpu.SemaphoreType.DMA]
    return pl.pallas_call(
        first_body if step == 0 else second_body,
        out_shape=[jax.ShapeDtypeStruct((count, cols), jnp.float32) for count in counts],
        in_specs=[smem, smem] + [vmem] * 10 + ([pl.BlockSpec(memory_space=pl.ANY)] if step == 0 else [vmem] * 2),
        out_specs=[vmem] * len(counts),
        scratch_shapes=scratch,
        compiler_params=pltpu.CompilerParams(vmem_limit_bytes=UPDATE_BYTES),
        cost_estimate=pl.CostEstimate(flops=6 * rows * depth * cols, bytes_accessed=4 * rows * (depth + 3 * cols), transcendentals=0),
        name="update",
    )(flags, slot_block, *pair, *blocks, *current)


def general(rows, cols, rhs, panel, diag_inverse, flags, slot_block):
    rank = lax.axis_index("row")
    owners = (jnp.argmax(slot_block == 0), jnp.argmax(slot_block == 1))
    weights = flags[0].astype(jnp.float32)
    bits = rows.bit_length() - 1
    current = rhs[0]
    solved = []
    for step in range(2):
        pivot = current
        for b in range(bits - 1):
            pivot = scatter_step(pivot, b, rows, owners[step], rank)
        pivot = cross_step(pivot, bits - 1, rows, owners[step], rank)
        for b in reversed(range(bits - 1)):
            pivot = gather_step(pivot, b, rows, rank)
        x = jnp.dot(diag_inverse[step], pivot, precision=HIGH)
        for b in range(bits):
            x = gather_step(x, b, rows, rank)
        whole = lax.all_gather(panel[0, step], "col", axis=0, tiled=True)
        current = current - weights[step] * jnp.dot(whole, x, precision=HIGH)
        solved.append(x)
    held = slot_block[rank]
    return jnp.where(held == 0, solved[0], jnp.where(held == 1, solved[1], current))[None]


def paced(rows, cols, rhs, panel, diag_inverse, flags, slot_block):
    rank = lax.axis_index("row")
    owner, second = jnp.argmax(slot_block == 0), jnp.argmax(slot_block == 1)
    half = panel.shape[2] // 2
    core = bit(rank, 0)

    def near(one, two):
        return [swap(one, "col", 0, cols), swap(two, "col", 1, cols)]

    def far(one, two):
        return [swap(one, "col", 1, cols), swap(two, "col", 0, cols)]

    def block_halves(panel, step):
        return panel[0, step, :half], panel[0, step, half:]

    def solved(step, y, panel, owner):
        y, panel = tie(y, panel)
        block = tie(*block_halves(panel, step))
        first = near(*block)
        y = scatter_step(y, 1, rows, owner, rank)
        y, *block = tie(y, *block)
        second = near(*block[::-1])
        y = cross_step(y, 2, rows, owner, rank)
        y, inverse, *first = tie(y, diag_inverse, *first)
        pieces = far(*first)
        beside = swap(y, "row", 1, rows)
        y, *second = tie(y, *second)
        other = swap(y, "row", 0, rows)
        beside, inverse = tie(beside, inverse[step])
        last = swap(beside, "row", 0, rows)
        x = solve(inverse, [y, beside, other, last])
        x2, x1 = swap(x, "row", 2, rows), swap(x, "row", 1, rows)
        x2, x1, *pieces = tie(x2, x1, *pieces)
        high, low = prepare([*block, *first, *second, *pieces])
        x3 = swap(x2, "row", 1, rows)
        across = [swap(block, "row", 0, rows) for block in (x, x1, x2)]
        x3, high, low, *across = tie(x3, high, low, *across)
        return [x, x1, x2, x3, *across, swap(x3, "row", 0, rows)], (high, low)

    got = swap(rhs, "row", 0, rows)
    kept, owner = tie(rhs, owner)
    keep, owner = tie(halves(kept[0], core)[0], owner)
    y = jnp.where(bit(owner, 0) == core, keep, halves(got[0], core)[0])
    blocks, pair = solved(0, y, panel, owner)
    keep, send = update(0, flags, slot_block, pair, blocks, [rhs])
    got = swap(send, "row", 0, rows)
    y = jnp.where(bit(second, 0) == core, keep, got)
    blocks, pair = solved(1, y, panel, second)
    (result,) = update(1, flags, slot_block, pair, blocks, [keep, send])
    return result[None]


def solution(mesh):
    rows, cols = mesh.shape["row"], mesh.shape["col"]
    form = paced if (rows, cols) == (8, 4) else general

    def shards(*args):
        return form(rows, cols, *args)

    in_specs = (
        P("row", None, "col"),
        P("row", None, "col", None),
        P(None, "row", None),
        P("row", None),
        P(),
    )
    out_specs = P("row", None, "col")
    return jax.shard_map(shards, mesh=mesh, in_specs=in_specs, out_specs=out_specs, check_vma=False)
```
